128 devices in a mesh: row: 8 (over y_lo, z), col: 16 (over x, y_hi, core).
Axes of the slice: x: 4, y: 4 (y_hi: 2, y_lo: 2; y = y_hi * 2 + y_lo), z: 4, core: 2. Of those that a mesh axis runs over, the one named last changes fastest.
Arguments:
- pair: float32 [512, 1024, 128], P('row', 'col'), may hold values from -6 to 6
- right_proj: bfloat16 [64, 1024, 1024], P(None, 'row', 'col'), may hold values from -3 to 3
- w_left_gate: bfloat16 [128, 64], replicated, may hold values from -0.5 to 0.5
- w_left: bfloat16 [128, 64], replicated, may hold values from -0.5 to 0.5
- w_gate: bfloat16 [128, 128], replicated, may hold values from -0.5 to 0.5
- out_gain: float32 [64], replicated, may hold values from 0.1 to 1.9
- w_out: bfloat16 [64, 128], replicated, may hold values from -0.75 to 0.75
- cotangent: float32 [512, 1024, 128], P('row', 'col'), may hold values from -6 to 6
Outputs:
- update: float32 [512, 1024, 128], P('row', 'col')
- grad_pair: float32 [512, 1024, 128], P('row', 'col')
- grad_right: bfloat16 [64, 1024, 1024], P(None, 'row', 'col')
The draws below stay inside these ranges and needn't reach their ends.
All inputs are finite; a program needn't handle non-finite values.
Results may differ from the reference program's by a relative error of at most 0.02.
Values may be sent and summed in bfloat16 or wider, within the bound.
A program may use at most 192 MiB of HBM per device.

```python
import jax
import jax.numpy as jnp
from jax import lax

CH = 128
HID = 64
ROWS = 512
RES = 1024
N_COL = 16


def steps_of(stream_key, dims, cuts, smallest, largest):
    def one(dim, shards_of):
        steps = jax.random.uniform(jax.random.fold_in(jax.random.fold_in(stream_key, 6), dim), (shards_of,), jnp.float32, smallest / len(cuts), largest / len(cuts))
        return jnp.repeat(jnp.exp(steps), dims[dim] // shards_of).reshape((-1,) + (1,) * (len(dims) - dim - 1))

    factor_of = one(*cuts[0])
    for cut in cuts[1:]:
        factor_of = factor_of * one(*cut)
    return factor_of


def noise(rng, dims, scale, bound, shards=(), dtype=jnp.bfloat16):
    factor_of = steps_of(rng, dims, shards, -0.22, 0.18) if shards else 1.0
    result = jax.random.normal(rng, dims, jnp.float32) * scale * factor_of
    return jnp.minimum(jnp.maximum(result, -bound), bound).astype(dtype)


def setup_inputs(seed: int = 0) -> dict:
    arg_keys = jax.random.split(jax.random.key(seed), 9)
    pair = noise(arg_keys[0], (ROWS, RES, CH), 1.0, 6.0, ((0, 8), (1, 16)), jnp.float32)
    right_proj = noise(arg_keys[1], (HID, RES, RES), 0.5, 3.0, ((1, 8), (2, 16)))
    w_left_gate = noise(arg_keys[2], (CH, HID), CH ** -0.5, 0.5)
    w_left = noise(arg_keys[3], (CH, HID), CH ** -0.5, 0.5)
    w_gate = noise(arg_keys[4], (CH, CH), CH ** -0.5, 0.5)
    out_gain = jnp.clip(1.0 + 0.18 * jax.random.normal(arg_keys[5], (HID,), jnp.float32), 0.1, 1.9)
    w_out = noise(arg_keys[6], (HID, CH), HID ** -0.5, 0.75)
    cotangent = noise(arg_keys[7], (ROWS, RES, CH), 1.0, 6.0, ((0, 8), (1, 16)), jnp.float32)
    return {"pair": pair, "right_proj": right_proj, "w_left_gate": w_left_gate, "w_left": w_left, "w_gate": w_gate, "out_gain": out_gain, "w_out": w_out, "cotangent": cotangent}


EPS = 1e-05

def normalize(values):
    centred = values - lax.optimization_barrier(jnp.mean(values, -1, keepdims=True))
    inv_std = lax.rsqrt(lax.optimization_barrier(jnp.mean(centred * centred, -1, keepdims=True)) + EPS)
    return (centred * inv_std, inv_std)

def norm_back(grad, normed, inv_std):
    return inv_std * (grad - lax.optimization_barrier(jnp.mean(grad, -1, keepdims=True)) - normed * lax.optimization_barrier(jnp.mean(grad * normed, -1, keepdims=True)))

def reference(pair, right_proj, w_left_gate, w_left, w_gate, out_gain, w_out, cotangent):
    highest = lax.Precision.HIGHEST
    normed, inv_in = normalize(pair)
    normed_low = normed.astype(jnp.bfloat16)
    left_logit = jnp.dot(normed_low, w_left_gate, preferred_element_type=jnp.float32)
    left_value = jnp.dot(normed_low, w_left, preferred_element_type=jnp.float32)
    left_sig = jax.nn.sigmoid(left_logit)
    left_low = (left_sig * left_value).astype(jnp.bfloat16)
    left_heads = jnp.transpose(left_low, (2, 0, 1)).astype(jnp.float32)
    right_wide = right_proj.astype(jnp.float32)
    triangle = jnp.einsum('hik,hkj->ijh', left_heads, right_wide, precision=highest)
    tri_hat, inv_out = normalize(triangle)
    tri_low = (tri_hat * out_gain).astype(jnp.bfloat16)
    linear = jnp.dot(tri_low, w_out, preferred_element_type=jnp.float32)
    gate = jax.nn.sigmoid(jnp.dot(normed_low, w_gate, preferred_element_type=jnp.float32))
    update = gate * linear
    d_linear = cotangent * gate
    d_gate = cotangent * linear * gate * (1.0 - gate)
    d_scaled = jnp.dot(d_linear.astype(jnp.bfloat16), w_out.T, preferred_element_type=jnp.float32) * out_gain
    d_tri = norm_back(d_scaled, tri_hat, inv_out).astype(jnp.bfloat16)
    grad_heads = jnp.transpose(d_tri, (2, 0, 1)).astype(jnp.float32)
    width = RES // N_COL
    grad_blocks = jnp.moveaxis(grad_heads.reshape(HID, ROWS, N_COL, width), 2, 0)
    right_blocks = jnp.moveaxis(right_wide.reshape(HID, RES, N_COL, width), 2, 0)

    def add_block(total, pieces):
        part = jnp.einsum('hij,hkj->ikh', pieces[0], pieces[1], precision=highest)
        part = lax.optimization_barrier(part.astype(jnp.bfloat16)).astype(jnp.float32)
        return (total + part, None)
    d_left, _ = lax.scan(add_block, jnp.zeros((ROWS, RES, HID), jnp.float32), (grad_blocks, right_blocks))
    grad_right = jnp.einsum('hik,hij->hkj', left_heads, grad_heads, precision=highest).astype(jnp.bfloat16)
    d_value = d_left * left_sig
    d_logit = d_left * left_value * left_sig * (1.0 - left_sig)
    stacked = jnp.concatenate([d_value, d_logit, d_gate], -1).astype(jnp.bfloat16)
    weights = jnp.concatenate([w_left, w_left_gate, w_gate], 1)
    d_normed = jnp.dot(stacked, weights.T, preferred_element_type=jnp.float32)
    grad_pair = norm_back(d_normed, normed, inv_in)
    return (update, grad_pair, grad_right)
```

```python
import functools

import jax
import jax.numpy as jnp
from jax import lax
from jax.experimental import pallas as pl
from jax.experimental.pallas import tpu as pltpu
from jax.sharding import PartitionSpec as P

EPS = 1e-05
F32 = jnp.float32
BF16 = jnp.bfloat16
MESH = pl.DeviceIdType.MESH

CH = 128
HID = 64
SIDE = 64
ROW = 8
COLC = 8
HALF = SIDE // 2
KB = 128
LANES = 128
PEERS = ROW * COLC


def dot(a, b, da, db):
    return lax.dot_general(a, b, (((da,), (db,)), ((), ())), preferred_element_type=F32)


def swap(a, b):
    left = lax.broadcasted_iota(jnp.int32, a.shape, a.ndim - 1) < LANES // 2
    ra = pltpu.roll(a, LANES // 2, a.ndim - 1)
    rb = pltpu.roll(b, LANES // 2, b.ndim - 1)
    return jnp.where(left, a, rb), jnp.where(left, ra, b)


def kernel(
    pair_hbm, right_hbm, wlg_ref, wl_ref, wg_ref, gain_ref, wo_ref, cot_hbm,
    upd_hbm, gp_hbm, gr_hbm,
    xn, cot, inv, gate, sig, val, dgate, upd,
    stage, send8, lb, lfull, rt, tm, tr, dtr, dtfull, grs, dlk, dlx, dly, dls, dlr, wcat, gcol,
    io_sem, send_sem, recv_sem,
):
    row, col = lax.axis_index("row"), lax.axis_index("col")
    core = lax.rem(col, 2)
    colc = col // 2
    me = row * COLC + colc
    sibling = (row, colc * 2 + (1 - core))

    def peer(off):
        prow = lax.rem(row + off // COLC, ROW)
        pcol = lax.rem(colc + lax.rem(off, COLC), COLC)
        return prow * COLC + pcol, (prow, pcol * 2 + core)

    load_pair = pltpu.make_async_copy(pair_hbm, xn, io_sem.at[0])
    load_pair.start()
    load_cot = pltpu.make_async_copy(cot_hbm, cot, io_sem.at[1])
    load_cot.start()

    barrier = pltpu.get_barrier_semaphore()

    def greet(off, _):
        pl.semaphore_signal(barrier, inc=1, device_id=peer(off)[1], device_id_type=MESH)
        return 0

    lax.fori_loop(1, PEERS, greet, 0)
    pl.semaphore_signal(barrier, inc=1, device_id=sibling, device_id_type=MESH)
    pl.semaphore_wait(barrier, PEERS)

    def exchange(src_of, dst, phase):
        pltpu.make_async_copy(src_of(me), dst, recv_sem.at[phase]).start()

        def one(off, _):
            q, device = peer(off)
            pltpu.make_async_remote_copy(
                src_ref=src_of(q),
                dst_ref=dst,
                send_sem=send_sem.at[phase],
                recv_sem=recv_sem.at[phase],
                device_id=device,
                device_id_type=MESH,
            ).start()
            return 0

        lax.fori_loop(1, PEERS, one, 0)

    def arrived(buf, phase):
        pltpu.make_async_copy(buf, buf, recv_sem.at[phase]).wait()

    def sent(buf, phase):
        part = buf.at[pl.ds(0, PEERS - 1)]
        pltpu.make_async_copy(part, part, send_sem.at[phase]).wait()

    exchange(lambda q: right_hbm.at[q], rt.at[row * COLC + colc], 0)

    wcat[:HID] = wl_ref[...]
    wcat[HID:] = wlg_ref[...]
    eye = lax.broadcasted_iota(jnp.int32, (HID, HID), 0) == lax.broadcasted_iota(jnp.int32, (HID, HID), 1)
    column = jnp.sum(jnp.where(eye, gain_ref[...], 0.0), axis=1, keepdims=True)
    gcol[...] = jnp.broadcast_to(column, (HID, LANES))

    load_pair.wait()

    def left_step(s, _):
        x = jnp.concatenate([xn[s], xn[s + HALF]], axis=0)
        centred = x - jnp.mean(x, -1, keepdims=True)
        inv_std = lax.rsqrt(jnp.mean(centred * centred, -1, keepdims=True) + EPS)
        normed = centred * inv_std
        xn[s] = normed[:SIDE]
        xn[s + HALF] = normed[SIDE:]
        inv[s] = jnp.broadcast_to(inv_std, (LANES, CH))
        low = normed.astype(BF16)
        both = dot(wcat[...], low, 1, 1)
        value = both[:HID]
        left_sig = jax.nn.sigmoid(both[HID:])
        val[s] = value
        sig[s] = left_sig
        stage[pl.ds(s, HID, stride=HALF), :] = left_sig * value
        return 0

    lax.fori_loop(0, HALF, left_step, 0, unroll=2)

    def pack(h, _):
        send8[h] = stage[pl.ds(h * HALF, HALF), :].astype(BF16)
        return 0

    lax.fori_loop(0, HID, pack, 0, unroll=4)
    exchange(lambda q: send8.at[q], lb.at[core, me], 1)

    def gate_step(s, _):
        low = jnp.concatenate([xn[s], xn[s + HALF]], axis=0).astype(BF16)
        gate[s] = jax.nn.sigmoid(dot(low, wg_ref[...], 1, 0))
        return 0

    lax.fori_loop(0, HALF, gate_step, 0, unroll=2)

    arrived(lb.at[core], 1)
    swap_left = pltpu.make_async_remote_copy(
        src_ref=lb.at[core],
        dst_ref=lb.at[core],
        send_sem=send_sem.at[2],
        recv_sem=recv_sem.at[2],
        device_id=sibling,
        device_id_type=MESH,
    )
    swap_left.start()
    arrived(lb.at[1 - core], 2)

    def unpack_left(q, _):
        r, c = q // COLC, lax.rem(q, COLC)
        top, bottom = swap(lb[0, q].astype(F32), lb[1, q].astype(F32))
        block = jnp.concatenate([top, bottom], axis=0).astype(BF16)
        lfull[c, pl.ds(pl.multiple_of(r * SIDE, SIDE), SIDE), :] = block
        return 0

    lax.fori_loop(0, PEERS, unpack_left, 0, unroll=2)

    def k_left(lo, rows=slice(None)):
        return jnp.concatenate([lfull[lo, rows], lfull[lo + 1, rows]], axis=1)

    def k_right(lo):
        a = jnp.concatenate([rt[lo * COLC + c] for c in range(COLC)], axis=0)
        b = jnp.concatenate([rt[(lo + 1) * COLC + c] for c in range(COLC)], axis=0)
        return jnp.concatenate([a, b], axis=1)

    arrived(rt, 0)

    TI = 256

    def triangle_step(t, _):
        rows = pl.ds(pl.multiple_of(t * TI, TI), TI)
        total = dot(k_left(0, rows), k_right(0), 1, 1)
        for lo in range(2, ROW, 2):
            total += dot(k_left(lo, rows), k_right(lo), 1, 1)
        for rr in range(TI // SIDE):
            for p in range(COLC // 2):
                lanes = slice(p * LANES, (p + 1) * LANES)
                a, b = swap(
                    total[rr * SIDE : rr * SIDE + HALF, lanes],
                    total[rr * SIDE + HALF : (rr + 1) * SIDE, lanes],
                )
                at = (t * (TI // SIDE) + rr) * COLC + 2 * p
                tm[at] = a.astype(BF16)
                tm[at + 1] = b.astype(BF16)
        return 0

    lax.fori_loop(0, ROW * SIDE // TI, triangle_step, 0)
    exchange(lambda q: tm.at[q], tr.at[me], 3)

    sent(send8, 1)
    arrived(tr, 3)

    def widen(buf):
        def one(h, _):
            stage[pl.ds(pl.multiple_of(h * HALF, HALF), HALF), :] = buf[h].astype(F32)
            return 0

        lax.fori_loop(0, HID, one, 0, unroll=4)

    widen(tr)
    load_cot.wait()

    def middle_step(s, _):
        tri = stage[pl.ds(s, HID, stride=HALF), :]
        centred = tri - jnp.mean(tri, 0, keepdims=True)
        inv_out = lax.rsqrt(jnp.mean(centred * centred, 0, keepdims=True) + EPS)
        hat = centred * inv_out
        gain = gcol[...]
        linear = dot((hat * gain).astype(BF16), wo_ref[...], 0, 0)
        g = gate[s]
        update = g * linear
        upd[s] = update[:SIDE]
        upd[s + HALF] = update[SIDE:]
        ct = jnp.concatenate([cot[s], cot[s + HALF]], axis=0)
        d_linear = ct * g
        dgate[s] = (ct * linear * g * (1.0 - g)).astype(BF16)
        d_scaled = dot(wo_ref[...], d_linear.astype(BF16), 1, 1) * gain
        d_tri = inv_out * (
            d_scaled
            - jnp.mean(d_scaled, 0, keepdims=True)
            - hat * jnp.mean(d_scaled * hat, 0, keepdims=True)
        )
        stage[pl.ds(s, HID, stride=HALF), :] = d_tri
        return 0

    lax.fori_loop(0, HALF, middle_step, 0, unroll=2)
    lax.fori_loop(0, HID, pack, 0, unroll=4)
    exchange(lambda q: send8.at[q], dtr.at[me], 4)
    store_upd = pltpu.make_async_copy(upd, upd_hbm, io_sem.at[2])
    store_upd.start()

    arrived(dtr, 4)

    def unpack_tri(n, _):
        r, p = n // (COLC // 2), lax.rem(n, COLC // 2)
        at = r * COLC + 2 * p
        top, bottom = swap(dtr[at].astype(F32), dtr[at + 1].astype(F32))
        block = jnp.concatenate([top, bottom], axis=0).astype(BF16)
        dtfull[p, pl.ds(pl.multiple_of(r * SIDE, SIDE), SIDE), :] = block
        return 0

    lax.fori_loop(0, PEERS // 2, unpack_tri, 0, unroll=2)
    d_tri_all = jnp.concatenate([dtfull[p] for p in range(COLC // 2)], axis=1)

    for lo in range(0, ROW, 2):
        part = dot(d_tri_all, k_right(lo), 1, 0)
        for c in range(2):
            for r in range(ROW):
                lanes = slice(c * LANES, (c + 1) * LANES)
                for_0, for_1 = swap(
                    part[r * SIDE : r * SIDE + HALF, lanes],
                    part[r * SIDE + HALF : (r + 1) * SIDE, lanes],
                )
                at = r * COLC + lo + c
                first = core == 0
                dlk[at] = jnp.where(first, for_0, for_1)
                dlx[at] = jnp.where(first, for_1, for_0).astype(BF16)
    swap_grad = pltpu.make_async_remote_copy(
        src_ref=dlx,
        dst_ref=dly,
        send_sem=send_sem.at[5],
        recv_sem=recv_sem.at[5],
        device_id=sibling,
        device_id_type=MESH,
    )
    swap_grad.start()

    for lo in range(0, COLC, 2):
        part = dot(d_tri_all, k_left(lo), 0, 0).astype(BF16)
        for c in range(2):
            for cc in range(COLC):
                grs[(lo + c) * COLC + cc] = part[cc * SIDE : (cc + 1) * SIDE, c * LANES : (c + 1) * LANES]

    swap_grad.wait_recv()

    def add_halves(q, _):
        dls[q] = (dlk[q] + dly[q].astype(F32)).astype(BF16)
        return 0

    lax.fori_loop(0, PEERS, add_halves, 0, unroll=4)
    exchange(lambda q: dls.at[q], dlr.at[me], 6)
    exchange(lambda q: grs.at[q], gr_hbm.at[me], 7)

    arrived(dlr, 6)
    widen(dlr)

    def final_step(s, _):
        d_left = stage[pl.ds(s, HID, stride=HALF), :]
        left_sig, value = sig[s], val[s]
        d_value = d_left * left_sig
        d_logit = d_left * value * left_sig * (1.0 - left_sig)
        stacked = jnp.concatenate([d_value, d_logit], axis=0).astype(BF16)
        grad = dot(stacked, wcat[...], 0, 0) + dot(dgate[s], wg_ref[...], 1, 1)
        normed = jnp.concatenate([xn[s], xn[s + HALF]], axis=0)
        out = inv[s] * (
            grad
            - jnp.mean(grad, -1, keepdims=True)
            - normed * jnp.mean(grad * normed, -1, keepdims=True)
        )
        xn[s] = out[:SIDE]
        xn[s + HALF] = out[SIDE:]
        return 0

    lax.fori_loop(0, HALF, final_step, 0, unroll=2)
    store_gp = pltpu.make_async_copy(xn, gp_hbm, io_sem.at[3])
    store_gp.start()

    sent(right_hbm, 0)
    swap_left.wait_send()
    sent(tm, 3)
    sent(send8, 4)
    swap_grad.wait_send()
    sent(dls, 6)
    sent(grs, 7)
    store_upd.wait()
    arrived(gr_hbm, 7)
    store_gp.wait()


def shards(pair, right_proj, w_left_gate, w_left, w_gate, out_gain, w_out, cotangent):
    any_spec = pl.BlockSpec(memory_space=pl.ANY)
    vmem = pl.BlockSpec(memory_space=pltpu.VMEM)
    cells = (SIDE, SIDE, CH)
    block8 = (PEERS, HALF, LANES)
    block16 = (PEERS, SIDE, KB)
    per_step = (HALF, LANES, CH)
    heads = (HALF, HID, LANES)
    scratch = [
        (cells, F32), (cells, F32), (per_step, F32), (per_step, F32), (heads, F32), (heads, F32),
        (per_step, BF16), (cells, F32),
        ((HID * HALF, LANES), F32),
        (block8, BF16),
        ((2,) + block8, BF16),
        ((COLC, ROW * SIDE, LANES), BF16),
        (block16, BF16),
        (block8, BF16),
        (block8, BF16),
        (block8, BF16),
        ((COLC // 2, ROW * SIDE, LANES), BF16),
        (block16, BF16),
        (block8, F32),
        (block8, BF16), (block8, BF16), (block8, BF16), (block8, BF16),
        ((2 * HID, CH), BF16),
        ((HID, LANES), F32),
    ]
    update, grad_pair, grad_right = pl.pallas_call(
        kernel,
        out_shape=(
            jax.ShapeDtypeStruct(cells, F32),
            jax.ShapeDtypeStruct(cells, F32),
            jax.ShapeDtypeStruct((HID, SIDE, KB), BF16),
        ),
        in_specs=[any_spec, any_spec, vmem, vmem, vmem, vmem, vmem, any_spec],
        out_specs=(any_spec, any_spec, any_spec),
        scratch_shapes=[pltpu.VMEM(shape, dtype) for shape, dtype in scratch]
        + [
            pltpu.SemaphoreType.DMA((4,)),
            pltpu.SemaphoreType.DMA((8,)),
            pltpu.SemaphoreType.DMA((8,)),
        ],
        compiler_params=pltpu.CompilerParams(
            collective_id=0, has_side_effects=True, vmem_limit_bytes=56 * 1024 * 1024
        ),
    )(
        pair,
        jnp.transpose(right_proj, (0, 2, 1)),
        w_left_gate.T,
        w_left.T,
        w_gate,
        out_gain.reshape(1, HID),
        w_out,
        cotangent,
    )
    return update, grad_pair, jnp.transpose(grad_right, (0, 2, 1))


def solution(mesh):
    in_specs = (
        P("row", "col", None),
        P(None, "row", "col"),
        P(),
        P(),
        P(),
        P(),
        P(),
        P("row", "col", None),
    )
    out_specs = (P("row", "col", None), P("row", "col", None), P(None, "row", "col"))
    return jax.shard_map(shards, mesh=mesh, in_specs=in_specs, out_specs=out_specs, check_vma=False)
```

```python
import functools

import jax
import jax.numpy as jnp
from jax import lax
from jax.experimental import pallas as pl
from jax.experimental.pallas import tpu as pltpu
from jax.sharding import PartitionSpec as P

EPS = 1e-05
F32 = jnp.float32
BF16 = jnp.bfloat16
MESH = pl.DeviceIdType.MESH

CH = 128
HID = 64
SIDE = 64
ROW = 8
COLC = 8
HALF = SIDE // 2
KB = 128
LANES = 128
PEERS = ROW * COLC
NCH = 2
SB = HALF // NCH
TR = ROW * 2 * SB
UNROLL = 2


def dot(a, b, da, db):
    return lax.dot_general(a, b, (((da,), (db,)), ((), ())), preferred_element_type=F32)


def swap(a, b):
    left = lax.broadcasted_iota(jnp.int32, a.shape, a.ndim - 1) < LANES // 2
    ra = pltpu.roll(a, LANES // 2, a.ndim - 1)
    rb = pltpu.roll(b, LANES // 2, b.ndim - 1)
    return jnp.where(left, a, rb), jnp.where(left, ra, b)


def kernel(
    pair_hbm, right_hbm, wlg_ref, wl_ref, wg_ref, gain_ref, wo_ref, cot_hbm,
    upd, gp, gr,
    xn, cot, inv, gate, sig, val, dgate,
    stage, send_l, lb, lfull, rt, tm, tr, dts, dtr, dtfull, grs, dlk, dlx, dly, dls, dlr, wcat, gcol,
    io_sem, send_sem, recv_sem, tri_sem, stage_sem,
):
    row, col = lax.axis_index("row"), lax.axis_index("col")
    core = lax.rem(col, 2)
    colc = col // 2
    me = row * COLC + colc
    sibling = (row, colc * 2 + (1 - core))

    def peer(off):
        prow = lax.rem(row + off // COLC, ROW)
        pcol = lax.rem(colc + lax.rem(off, COLC), COLC)
        return prow * COLC + pcol, (prow, pcol * 2 + core)

    load_pair = pltpu.make_async_copy(pair_hbm, xn, io_sem.at[0])
    load_pair.start()
    load_cot = pltpu.make_async_copy(cot_hbm, cot, io_sem.at[1])
    load_cot.start()

    barrier = pltpu.get_barrier_semaphore()

    def greet(off, _):
        pl.semaphore_signal(barrier, inc=1, device_id=peer(off)[1], device_id_type=MESH)
        pl.semaphore_signal(barrier, inc=1, device_id=peer(off * COLC)[1], device_id_type=MESH)
        return 0

    def greet_again(off, _):
        pl.semaphore_signal(stage_sem, inc=1, device_id=peer(off * COLC)[1], device_id_type=MESH)
        return 0

    lax.fori_loop(1, ROW, greet, 0)
    pl.semaphore_signal(barrier, inc=1, device_id=sibling, device_id_type=MESH)

    def exchange(src_of, dst, send, recv, lo=1, hi=PEERS):
        if lo == 1:
            pltpu.make_async_copy(src_of(me), dst, recv).start()

        def one(off, _):
            q, device = peer(off)
            pltpu.make_async_remote_copy(
                src_ref=src_of(q),
                dst_ref=dst,
                send_sem=send,
                recv_sem=recv,
                device_id=device,
                device_id_type=MESH,
            ).start()
            return 0

        lax.fori_loop(lo, hi, one, 0)

    def arrived(buf, sem):
        pltpu.make_async_copy(buf, buf, sem).wait()

    def sent(buf, sem):
        part = buf.at[pl.ds(0, PEERS - 1)]
        pltpu.make_async_copy(part, part, sem).wait()

    wcat[:HID] = wl_ref[...]
    wcat[HID:] = wlg_ref[...]
    eye = lax.broadcasted_iota(jnp.int32, (HID, HID), 0) == lax.broadcasted_iota(jnp.int32, (HID, HID), 1)
    column = jnp.sum(jnp.where(eye, gain_ref[...], 0.0), axis=1, keepdims=True)
    gcol[...] = jnp.broadcast_to(column, (HID, LANES))

    load_pair.wait()

    def stage_rows(s):
        return pl.ds((s // SB) * (HID * SB) + lax.rem(s, SB), HID, stride=SB)

    def left_step(s, _):
        x = jnp.concatenate([xn[s], xn[s + HALF]], axis=0)
        centred = x - jnp.mean(x, -1, keepdims=True)
        inv_std = lax.rsqrt(jnp.mean(centred * centred, -1, keepdims=True) + EPS)
        normed = centred * inv_std
        xn[s] = normed[:SIDE]
        xn[s + HALF] = normed[SIDE:]
        inv[s] = jnp.broadcast_to(inv_std, (LANES, CH))
        both = dot(wcat[...], normed.astype(BF16), 1, 1)
        value = both[:HID]
        left_sig = jax.nn.sigmoid(both[HID:])
        val[s] = value
        sig[s] = left_sig
        stage[stage_rows(s), :] = left_sig * value
        return 0

    lax.fori_loop(0, SB, left_step, 0, unroll=UNROLL)
    pl.semaphore_wait(barrier, 2 * ROW - 1)
    lax.fori_loop(1, ROW, greet_again, 0)
    lax.fori_loop(SB, HALF, left_step, 0, unroll=UNROLL)

    def stage_block(t, h):
        return pl.ds(pl.multiple_of((t * HID + h) * SB, SB), SB)

    def pack_left(h, _):
        send_l[h] = jnp.concatenate([stage[stage_block(t, h), :] for t in range(NCH)], axis=0).astype(BF16)
        return 0

    lax.fori_loop(0, HID, pack_left, 0, unroll=4)
    pl.semaphore_wait(stage_sem, ROW - 1)
    exchange(lambda q: send_l.at[q], lb.at[core, me], send_sem.at[1], recv_sem.at[1])
    exchange(lambda q: right_hbm.at[q], rt.at[me], send_sem.at[0], recv_sem.at[0])

    def gate_step(s, _):
        low = jnp.concatenate([xn[s], xn[s + HALF]], axis=0).astype(BF16)
        gate[s] = jax.nn.sigmoid(dot(low, wg_ref[...], 1, 0))
        return 0

    lax.fori_loop(0, HALF, gate_step, 0, unroll=UNROLL)

    arrived(lb.at[core], recv_sem.at[1])
    swap_left = pltpu.make_async_remote_copy(
        src_ref=lb.at[core],
        dst_ref=lb.at[core],
        send_sem=send_sem.at[2],
        recv_sem=recv_sem.at[2],
        device_id=sibling,
        device_id_type=MESH,
    )
    swap_left.start()
    arrived(lb.at[1 - core], recv_sem.at[2])

    def unpack_left(q, _):
        r, c = q // COLC, lax.rem(q, COLC)
        top, bottom = swap(lb[0, q].astype(F32), lb[1, q].astype(F32))
        for t in range(NCH):
            block = jnp.concatenate([top[t * SB : (t + 1) * SB], bottom[t * SB : (t + 1) * SB]], axis=0)
            at = pl.multiple_of(t * TR + r * 2 * SB, 2 * SB)
            lfull[c, pl.ds(at, 2 * SB), :] = block.astype(BF16)
        return 0

    lax.fori_loop(0, PEERS, unpack_left, 0, unroll=2)

    def k_left(lo, rows=slice(None)):
        return jnp.concatenate([lfull[lo, rows], lfull[lo + 1, rows]], axis=1)

    def k_right(lo):
        a = jnp.concatenate([rt[lo * COLC + c] for c in range(COLC)], axis=0)
        b = jnp.concatenate([rt[(lo + 1) * COLC + c] for c in range(COLC)], axis=0)
        return jnp.concatenate([a, b], axis=1)

    arrived(rt, recv_sem.at[0])

    for t in range(NCH):
        rows = slice(t * TR, (t + 1) * TR)
        total = dot(k_left(0, rows), k_right(0), 1, 1)
        for lo in range(2, ROW, 2):
            total += dot(k_left(lo, rows), k_right(lo), 1, 1)
        for r in range(ROW):
            for p in range(COLC // 2):
                lanes = slice(p * LANES, (p + 1) * LANES)
                a, b = swap(
                    total[r * 2 * SB : r * 2 * SB + SB, lanes],
                    total[r * 2 * SB + SB : (r + 1) * 2 * SB, lanes],
                )
                tm[t, r * COLC + 2 * p] = a.astype(BF16)
                tm[t, r * COLC + 2 * p + 1] = b.astype(BF16)
        exchange(lambda q: tm.at[t, q], tr.at[t, me], tri_sem.at[0, t], tri_sem.at[1, t])

    def widen(buf, t):
        def one(h, _):
            stage[stage_block(t, h), :] = buf[t, h].astype(F32)
            return 0

        lax.fori_loop(0, HID, one, 0, unroll=8)

    def middle_step(s, _):
        tri = stage[stage_rows(s), :]
        centred = tri - jnp.mean(tri, 0, keepdims=True)
        inv_out = lax.rsqrt(jnp.mean(centred * centred, 0, keepdims=True) + EPS)
        hat = centred * inv_out
        gain = gcol[...]
        linear = dot((hat * gain).astype(BF16), wo_ref[...], 0, 0)
        g = gate[s]
        update = g * linear
        upd[s] = update[:SIDE]
        upd[s + HALF] = update[SIDE:]
        ct = jnp.concatenate([cot[s], cot[s + HALF]], axis=0)
        d_linear = ct * g
        dgate[s] = (ct * linear * g * (1.0 - g)).astype(BF16)
        d_scaled = dot(wo_ref[...], d_linear.astype(BF16), 1, 1) * gain
        d_tri = inv_out * (
            d_scaled
            - jnp.mean(d_scaled, 0, keepdims=True)
            - hat * jnp.mean(d_scaled * hat, 0, keepdims=True)
        )
        stage[stage_rows(s), :] = d_tri
        return 0

    load_cot.wait()
    for t in range(NCH):
        arrived(tr.at[t], tri_sem.at[1, t])
        widen(tr, t)
        lax.fori_loop(t * SB, (t + 1) * SB, middle_step, 0, unroll=UNROLL)

        def pack_tri(h, _):
            dts[t, h] = stage[stage_block(t, h), :].astype(BF16)
            return 0

        lax.fori_loop(0, HID, pack_tri, 0, unroll=8)
        exchange(lambda q: dts.at[t, q], dtr.at[t, me], tri_sem.at[2, t], tri_sem.at[3, t])

    def swap_grad(t):
        return pltpu.make_async_remote_copy(
            src_ref=dlx.at[t],
            dst_ref=dly.at[t],
            send_sem=tri_sem.at[4, t],
            recv_sem=tri_sem.at[5, t],
            device_id=sibling,
            device_id_type=MESH,
        )

    def left_grad(t):
        arrived(dtr.at[t], tri_sem.at[3, t])

        def unpack_tri(n, _):
            r, p = n // (COLC // 2), lax.rem(n, COLC // 2)
            at = r * COLC + 2 * p
            top, bottom = swap(dtr[t, at].astype(F32), dtr[t, at + 1].astype(F32))
            block = jnp.concatenate([top, bottom], axis=0).astype(BF16)
            dtfull[p, pl.ds(pl.multiple_of(t * TR + r * 2 * SB, 2 * SB), 2 * SB), :] = block
            return 0

        lax.fori_loop(0, PEERS // 2, unpack_tri, 0, unroll=4)
        d_tri = jnp.concatenate([dtfull[p, t * TR : (t + 1) * TR] for p in range(COLC // 2)], axis=1)
        for lo in range(0, ROW, 2):
            part = dot(d_tri, k_right(lo), 1, 0)
            for c in range(2):
                for r in range(ROW):
                    lanes = slice(c * LANES, (c + 1) * LANES)
                    for_0, for_1 = swap(
                        part[r * 2 * SB : r * 2 * SB + SB, lanes],
                        part[r * 2 * SB + SB : (r + 1) * 2 * SB, lanes],
                    )
                    at = r * COLC + lo + c
                    first = core == 0
                    dlk[t, at] = jnp.where(first, for_0, for_1)
                    dlx[t, at] = jnp.where(first, for_1, for_0).astype(BF16)
        swap_grad(t).start()

    def send_left_grad(t):
        swap_grad(t).wait_recv()

        def add_halves(q, _):
            dls[t, q] = (dlk[t, q] + dly[t, q].astype(F32)).astype(BF16)
            return 0

        lax.fori_loop(0, PEERS, add_halves, 0, unroll=8)
        exchange(lambda q: dls.at[t, q], dlr.at[t, me], tri_sem.at[6, t], tri_sem.at[7, t])

    for t in range(NCH - 1):
        left_grad(t)
        send_left_grad(t)
    left_grad(NCH - 1)

    d_tri_all = jnp.concatenate([dtfull[p] for p in range(COLC // 2)], axis=1)
    for lo in range(0, COLC, 2):
        part = dot(d_tri_all, k_left(lo), 0, 0).astype(BF16)
        for c in range(2):
            for cc in range(COLC):
                grs[(lo + c) * COLC + cc] = part[cc * SIDE : (cc + 1) * SIDE, c * LANES : (c + 1) * LANES]

    def send_right_grad(lo, hi):
        exchange(lambda q: grs.at[q], gr.at[me], send_sem.at[3], recv_sem.at[3], lo, hi)

    send_right_grad(1, PEERS // 2)
    send_left_grad(NCH - 1)
    send_right_grad(PEERS // 2, PEERS)

    def final_step(s, _):
        d_left = stage[stage_rows(s), :]
        left_sig, value = sig[s], val[s]
        d_value = d_left * left_sig
        d_logit = d_left * value * left_sig * (1.0 - left_sig)
        stacked = jnp.concatenate([d_value, d_logit], axis=0).astype(BF16)
        grad = dot(stacked, wcat[...], 0, 0) + dot(dgate[s], wg_ref[...], 1, 1)
        normed = jnp.concatenate([xn[s], xn[s + HALF]], axis=0)
        out = inv[s] * (
            grad
            - jnp.mean(grad, -1, keepdims=True)
            - normed * jnp.mean(grad * normed, -1, keepdims=True)
        )
        gp[s] = out[:SIDE]
        gp[s + HALF] = out[SIDE:]
        return 0

    for t in range(NCH):
        arrived(dlr.at[t], tri_sem.at[7, t])
        widen(dlr, t)
        lax.fori_loop(t * SB, (t + 1) * SB, final_step, 0, unroll=UNROLL)

    sent(right_hbm, send_sem.at[0])
    sent(send_l, send_sem.at[1])
    swap_left.wait_send()
    for t in range(NCH):
        sent(tm.at[t], tri_sem.at[0, t])
        sent(dts.at[t], tri_sem.at[2, t])
        swap_grad(t).wait_send()
        sent(dls.at[t], tri_sem.at[6, t])
    sent(grs, send_sem.at[3])
    arrived(gr, recv_sem.at[3])


def shards(pair, right_proj, w_left_gate, w_left, w_gate, out_gain, w_out, cotangent):
    any_spec = pl.BlockSpec(memory_space=pl.ANY)
    vmem = pl.BlockSpec(memory_space=pltpu.VMEM)
    cells = (SIDE, SIDE, CH)
    block8 = (PEERS, HALF, LANES)
    chunks = (NCH, PEERS, SB, LANES)
    block16 = (PEERS, SIDE, KB)
    per_step = (HALF, LANES, CH)
    heads = (HALF, HID, LANES)
    scratch = [
        (cells, F32), (cells, F32), (per_step, F32), (per_step, F32), (heads, F32), (heads, F32),
        (per_step, BF16),
        ((HID * HALF, LANES), F32),
        (block8, BF16),
        ((2,) + block8, BF16),
        ((COLC, ROW * SIDE, LANES), BF16),
        (block16, BF16),
        (chunks, BF16), (chunks, BF16), (chunks, BF16), (chunks, BF16),
        ((COLC // 2, ROW * SIDE, LANES), BF16),
        (block16, BF16),
        (chunks, F32),
        (chunks, BF16), (chunks, BF16), (chunks, BF16), (chunks, BF16),
        ((2 * HID, CH), BF16),
        ((HID, LANES), F32),
    ]
    update, grad_pair, grad_right = pl.pallas_call(
        kernel,
        out_shape=(pltpu.VMEM(cells, F32), pltpu.VMEM(cells, F32), pltpu.VMEM((HID, SIDE, KB), BF16)),
        in_specs=[any_spec, any_spec, vmem, vmem, vmem, vmem, vmem, any_spec],
        out_specs=(vmem, vmem, vmem),
        scratch_shapes=[pltpu.VMEM(shape, dtype) for shape, dtype in scratch]
        + [
            pltpu.SemaphoreType.DMA((2,)),
            pltpu.SemaphoreType.DMA((4,)),
            pltpu.SemaphoreType.DMA((4,)),
            pltpu.SemaphoreType.DMA((8, NCH)),
            pltpu.SemaphoreType.REGULAR,
        ],
        compiler_params=pltpu.CompilerParams(
            collective_id=0, has_side_effects=True, vmem_limit_bytes=58 * 1024 * 1024
        ),
    )(
        pair,
        jnp.transpose(right_proj, (0, 2, 1)),
        w_left_gate.T,
        w_left.T,
        w_gate,
        out_gain.reshape(1, HID),
        w_out,
        cotangent,
    )
    return update, grad_pair, jnp.transpose(grad_right, (0, 2, 1))


def solution(mesh):
    in_specs = (
        P("row", "col", None),
        P(None, "row", "col"),
        P(),
        P(),
        P(),
        P(),
        P(),
        P("row", "col", None),
    )
    out_specs = (P("row", "col", None), P("row", "col", None), P(None, "row", "col"))
    return jax.shard_map(shards, mesh=mesh, in_specs=in_specs, out_specs=out_specs, check_vma=False)
```

```python
import random

import jax
import jax.numpy as jnp
from jax import lax
from jax.experimental import pallas as pl
from jax.experimental.pallas import tpu as pltpu
from jax.sharding import PartitionSpec as P

EPS = 1e-05
F32 = jnp.float32
BF16 = jnp.bfloat16
MESH = pl.DeviceIdType.MESH

CH = 128
HID = 64
SIDE = 64
ROW = 8
COLC = 8
HALF = SIDE // 2
KB = 128
LANES = 128
PEERS = ROW * COLC
NCH = 2
SB = HALF // NCH
TR = ROW * 2 * SB
UNROLL = 8
STEPS = (0, 1, 2, -1)
OTHERS = [(x, y, z) for x in STEPS for y in STEPS for z in STEPS if (x, y, z) != (0, 0, 0)]
random.Random(1).shuffle(OTHERS)
OTHERS.sort(key=lambda v: -sum(map(abs, v)))
PLANE = [v for v in OTHERS if v[2] == 0]
LINE = [v for v in OTHERS if v[0] == 0 and v[1] == 0]
NEAR = [v for v in OTHERS if v in PLANE or v in LINE]
REST = [v for v in OTHERS if v not in NEAR]


def dot(a, b, da, db):
    return lax.dot_general(a, b, (((da,), (db,)), ((), ())), preferred_element_type=F32)


def swap(a, b):
    left = lax.broadcasted_iota(jnp.int32, a.shape, a.ndim - 1) < LANES // 2
    ra = pltpu.roll(a, LANES // 2, a.ndim - 1)
    rb = pltpu.roll(b, LANES // 2, b.ndim - 1)
    return jnp.where(left, a, rb), jnp.where(left, ra, b)


def kernel(
    pair_hbm, right_hbm, wlg_ref, wl_ref, wg_ref, gain_ref, wo_ref, cot_hbm,
    upd, gp, gr,
    xn, cot, inv, gate, sig, val, dgate,
    stage, send_l, lb, lfull, rt, tm, tr, dts, dtr, dtfull, grs, dlk, dlx, dly, dls, dlr, wcat, gcol,
    io_sem, send_sem, recv_sem, tri_sem, line_sem,
):
    row, col = lax.axis_index("row"), lax.axis_index("col")
    core = lax.rem(col, 2)
    colc = col // 2
    me = row * COLC + colc
    sibling = (row, colc * 2 + (1 - core))

    across = {d: lax.rem(colc // 2 + d + 4, 4) for d in STEPS}
    up = {d: lax.rem(lax.rem(colc, 2) * 2 + row // 4 + d + 4, 4) for d in STEPS}
    deep = {d: lax.rem(lax.rem(row, 4) + d + 4, 4) for d in STEPS}
    cols = {(x, y): across[x] * 2 + up[y] // 2 for x in STEPS for y in STEPS}
    rows_of = {(y, z): lax.rem(up[y], 2) * 4 + deep[z] for y in STEPS for z in STEPS}

    def peer(v):
        x, y, z = v
        prow, pcol = rows_of[y, z], cols[x, y]
        return prow * COLC + pcol, (prow, pcol * 2 + core)

    load_pair = pltpu.make_async_copy(pair_hbm, xn, io_sem.at[0])
    load_pair.start()
    load_cot = pltpu.make_async_copy(cot_hbm, cot, io_sem.at[1])
    load_cot.start()

    barrier = pltpu.get_barrier_semaphore()
    for v in NEAR:
        pl.semaphore_signal(barrier, inc=1, device_id=peer(v)[1], device_id_type=MESH)
    pl.semaphore_signal(barrier, inc=1, device_id=sibling, device_id_type=MESH)

    def keep(src_of, dst, recv):
        pltpu.make_async_copy(src_of(me), dst, recv).start()

    def exchange(src_of, dst, send, recv, others=OTHERS):
        for v in others:
            q, device = peer(v)
            pltpu.make_async_remote_copy(
                src_ref=src_of(q),
                dst_ref=dst,
                send_sem=send,
                recv_sem=recv,
                device_id=device,
                device_id_type=MESH,
            ).start()

    def arrived(buf, sem):
        pltpu.make_async_copy(buf, buf, sem).wait()

    def sent(buf, sem):
        part = buf.at[pl.ds(0, PEERS - 1)]
        pltpu.make_async_copy(part, part, sem).wait()

    wcat[:HID] = wl_ref[...]
    wcat[HID:] = wlg_ref[...]
    eye = lax.broadcasted_iota(jnp.int32, (HID, HID), 0) == lax.broadcasted_iota(jnp.int32, (HID, HID), 1)
    column = jnp.sum(jnp.where(eye, gain_ref[...], 0.0), axis=1, keepdims=True)
    gcol[...] = jnp.broadcast_to(column, (HID, LANES))

    load_pair.wait()

    def stage_rows(s):
        return pl.ds((s // SB) * (HID * SB) + lax.rem(s, SB), HID, stride=SB)

    def left_step(s, _):
        x = jnp.concatenate([xn[s], xn[s + HALF]], axis=0)
        centred = x - jnp.mean(x, -1, keepdims=True)
        inv_std = lax.rsqrt(jnp.mean(centred * centred, -1, keepdims=True) + EPS)
        normed = centred * inv_std
        xn[s] = normed[:SIDE]
        xn[s + HALF] = normed[SIDE:]
        inv[s] = jnp.broadcast_to(inv_std, (LANES, CH))
        both = dot(wcat[...], normed.astype(BF16), 1, 1)
        value = both[:HID]
        left_sig = jax.nn.sigmoid(both[HID:])
        val[s] = value
        sig[s] = left_sig
        stage[stage_rows(s), :] = left_sig * value
        return 0

    lax.fori_loop(0, SB, left_step, 0, unroll=UNROLL)
    pl.semaphore_wait(barrier, len(NEAR) + 1)
    for v in LINE:
        pl.semaphore_signal(line_sem, inc=1, device_id=peer(v)[1], device_id_type=MESH)

    def send_right(others):
        exchange(lambda q: right_hbm.at[q], rt.at[me], send_sem.at[0], recv_sem.at[0], others)

    keep(lambda q: right_hbm.at[q], rt.at[me], recv_sem.at[0])
    send_right(NEAR)
    lax.fori_loop(SB, HALF, left_step, 0, unroll=UNROLL)

    def stage_block(t, h):
        return pl.ds(pl.multiple_of((t * HID + h) * SB, SB), SB)

    def pack_left(h, _):
        send_l[h] = jnp.concatenate([stage[stage_block(t, h), :] for t in range(NCH)], axis=0).astype(BF16)
        return 0

    lax.fori_loop(0, HID, pack_left, 0, unroll=4)
    pl.semaphore_wait(line_sem, len(LINE))
    keep(lambda q: send_l.at[q], lb.at[core, me], recv_sem.at[1])
    exchange(lambda q: send_l.at[q], lb.at[core, me], send_sem.at[1], recv_sem.at[1])
    send_right(REST)

    def gate_step(s, _):
        low = jnp.concatenate([xn[s], xn[s + HALF]], axis=0).astype(BF16)
        gate[s] = jax.nn.sigmoid(dot(low, wg_ref[...], 1, 0))
        return 0

    lax.fori_loop(0, HALF, gate_step, 0, unroll=UNROLL)

    arrived(lb.at[core], recv_sem.at[1])
    swap_left = pltpu.make_async_remote_copy(
        src_ref=lb.at[core],
        dst_ref=lb.at[core],
        send_sem=send_sem.at[2],
        recv_sem=recv_sem.at[2],
        device_id=sibling,
        device_id_type=MESH,
    )
    swap_left.start()
    arrived(lb.at[1 - core], recv_sem.at[2])

    def unpack_left(q, _):
        r, c = q // COLC, lax.rem(q, COLC)
        top, bottom = swap(lb[0, q].astype(F32), lb[1, q].astype(F32))
        for t in range(NCH):
            block = jnp.concatenate([top[t * SB : (t + 1) * SB], bottom[t * SB : (t + 1) * SB]], axis=0)
            at = pl.multiple_of(t * TR + r * 2 * SB, 2 * SB)
            lfull[c, pl.ds(at, 2 * SB), :] = block.astype(BF16)
        return 0

    lax.fori_loop(0, PEERS, unpack_left, 0, unroll=4)

    def k_left(lo, rows=slice(None)):
        return jnp.concatenate([lfull[lo, rows], lfull[lo + 1, rows]], axis=1)

    def k_right(lo):
        a = jnp.concatenate([rt[lo * COLC + c] for c in range(COLC)], axis=0)
        b = jnp.concatenate([rt[(lo + 1) * COLC + c] for c in range(COLC)], axis=0)
        return jnp.concatenate([a, b], axis=1)

    arrived(rt, recv_sem.at[0])

    for t in range(NCH):
        rows = slice(t * TR, (t + 1) * TR)
        total = dot(k_left(0, rows), k_right(0), 1, 1)
        for lo in range(2, ROW, 2):
            total += dot(k_left(lo, rows), k_right(lo), 1, 1)
        for r in range(ROW):
            for p in range(COLC // 2):
                lanes = slice(p * LANES, (p + 1) * LANES)
                a, b = swap(
                    total[r * 2 * SB : r * 2 * SB + SB, lanes],
                    total[r * 2 * SB + SB : (r + 1) * 2 * SB, lanes],
                )
                tm[t, r * COLC + 2 * p] = a.astype(BF16)
                tm[t, r * COLC + 2 * p + 1] = b.astype(BF16)
        if t:
            sent(tm.at[t - 1], tri_sem.at[0, t - 1])
        keep(lambda q: tm.at[t, q], tr.at[t, me], tri_sem.at[1, t])
        exchange(lambda q: tm.at[t, q], tr.at[t, me], tri_sem.at[0, t], tri_sem.at[1, t])

    def widen(buf, t):
        def one(h, _):
            stage[stage_block(t, h), :] = buf[t, h].astype(F32)
            return 0

        lax.fori_loop(0, HID, one, 0, unroll=8)

    def middle_step(s, _):
        tri = stage[stage_rows(s), :]
        centred = tri - jnp.mean(tri, 0, keepdims=True)
        inv_out = lax.rsqrt(jnp.mean(centred * centred, 0, keepdims=True) + EPS)
        hat = centred * inv_out
        gain = gcol[...]
        linear = dot((hat * gain).astype(BF16), wo_ref[...], 0, 0)
        g = gate[s]
        update = g * linear
        upd[s] = update[:SIDE]
        upd[s + HALF] = update[SIDE:]
        ct = jnp.concatenate([cot[s], cot[s + HALF]], axis=0)
        d_linear = ct * g
        dgate[s] = (ct * linear * g * (1.0 - g)).astype(BF16)
        d_scaled = dot(wo_ref[...], d_linear.astype(BF16), 1, 1) * gain
        d_tri = inv_out * (
            d_scaled
            - jnp.mean(d_scaled, 0, keepdims=True)
            - hat * jnp.mean(d_scaled * hat, 0, keepdims=True)
        )
        stage[stage_rows(s), :] = d_tri
        return 0

    load_cot.wait()
    for t in range(NCH):
        arrived(tr.at[t], tri_sem.at[1, t])
        widen(tr, t)
        lax.fori_loop(t * SB, (t + 1) * SB, middle_step, 0, unroll=UNROLL)

        def pack_tri(h, _):
            dts[t, h] = stage[stage_block(t, h), :].astype(BF16)
            return 0

        lax.fori_loop(0, HID, pack_tri, 0, unroll=8)
        keep(lambda q: dts.at[t, q], dtr.at[t, me], tri_sem.at[3, t])
        exchange(lambda q: dts.at[t, q], dtr.at[t, me], tri_sem.at[2, t], tri_sem.at[3, t])

    def swap_grad(t):
        return pltpu.make_async_remote_copy(
            src_ref=dlx.at[t],
            dst_ref=dly.at[t],
            send_sem=tri_sem.at[4, t],
            recv_sem=tri_sem.at[5, t],
            device_id=sibling,
            device_id_type=MESH,
        )

    def tri_grad(t):
        arrived(dtr.at[t], tri_sem.at[3, t])

        def unpack_tri(n, _):
            r, p = n // (COLC // 2), lax.rem(n, COLC // 2)
            at = r * COLC + 2 * p
            top, bottom = swap(dtr[t, at].astype(F32), dtr[t, at + 1].astype(F32))
            block = jnp.concatenate([top, bottom], axis=0).astype(BF16)
            dtfull[p, pl.ds(pl.multiple_of(t * TR + r * 2 * SB, 2 * SB), 2 * SB), :] = block
            return 0

        lax.fori_loop(0, PEERS // 2, unpack_tri, 0, unroll=8)

    def left_grad(t):
        d_tri = jnp.concatenate([dtfull[p, t * TR : (t + 1) * TR] for p in range(COLC // 2)], axis=1)
        for lo in range(0, ROW, 2):
            part = dot(d_tri, k_right(lo), 1, 0)
            for c in range(2):
                for r in range(ROW):
                    lanes = slice(c * LANES, (c + 1) * LANES)
                    for_0, for_1 = swap(
                        part[r * 2 * SB : r * 2 * SB + SB, lanes],
                        part[r * 2 * SB + SB : (r + 1) * 2 * SB, lanes],
                    )
                    at = r * COLC + lo + c
                    first = core == 0
                    dlk[t, at] = jnp.where(first, for_0, for_1)
                    dlx[t, at] = jnp.where(first, for_1, for_0).astype(BF16)
        swap_grad(t).start()

    def send_left_grad(t):
        swap_grad(t).wait_recv()

        def add_halves(q, _):
            dls[t, q] = (dlk[t, q] + dly[t, q].astype(F32)).astype(BF16)
            return 0

        lax.fori_loop(0, PEERS, add_halves, 0, unroll=8)
        keep(lambda q: dls.at[t, q], dlr.at[t, me], tri_sem.at[7, t])
        exchange(lambda q: dls.at[t, q], dlr.at[t, me], tri_sem.at[6, t], tri_sem.at[7, t])

    for t in range(NCH - 1):
        tri_grad(t)
        left_grad(t)
        send_left_grad(t)
    tri_grad(NCH - 1)

    d_tri_all = jnp.concatenate([dtfull[p] for p in range(COLC // 2)], axis=1)
    for lo in range(0, COLC, 2):
        part = dot(d_tri_all, k_left(lo), 0, 0).astype(BF16)
        for c in range(2):
            for cc in range(COLC):
                grs[(lo + c) * COLC + cc] = part[cc * SIDE : (cc + 1) * SIDE, c * LANES : (c + 1) * LANES]

    def send_right_grad(others):
        exchange(lambda q: grs.at[q], gr.at[me], send_sem.at[3], recv_sem.at[3], others)

    keep(lambda q: grs.at[q], gr.at[me], recv_sem.at[3])
    send_right_grad(OTHERS[0::2])
    left_grad(NCH - 1)
    send_left_grad(NCH - 1)
    sent(dls.at[NCH - 1], tri_sem.at[6, NCH - 1])
    send_right_grad(OTHERS[1::2])

    def final_step(s, _):
        d_left = stage[stage_rows(s), :]
        left_sig, value = sig[s], val[s]
        d_value = d_left * left_sig
        d_logit = d_left * value * left_sig * (1.0 - left_sig)
        stacked = jnp.concatenate([d_value, d_logit], axis=0).astype(BF16)
        grad = dot(stacked, wcat[...], 0, 0) + dot(dgate[s], wg_ref[...], 1, 1)
        normed = jnp.concatenate([xn[s], xn[s + HALF]], axis=0)
        out = inv[s] * (
            grad
            - jnp.mean(grad, -1, keepdims=True)
            - normed * jnp.mean(grad * normed, -1, keepdims=True)
        )
        gp[s] = out[:SIDE]
        gp[s + HALF] = out[SIDE:]
        return 0

    for t in range(NCH):
        arrived(dlr.at[t], tri_sem.at[7, t])
        widen(dlr, t)
        lax.fori_loop(t * SB, (t + 1) * SB, final_step, 0, unroll=UNROLL)

    sent(right_hbm, send_sem.at[0])
    sent(send_l, send_sem.at[1])
    swap_left.wait_send()
    for t in range(NCH):
        sent(dts.at[t], tri_sem.at[2, t])
        swap_grad(t).wait_send()
    sent(tm.at[NCH - 1], tri_sem.at[0, NCH - 1])
    for t in range(NCH - 1):
        sent(dls.at[t], tri_sem.at[6, t])
    sent(grs, send_sem.at[3])
    arrived(gr, recv_sem.at[3])


def shards(pair, right_proj, w_left_gate, w_left, w_gate, out_gain, w_out, cotangent):
    any_spec = pl.BlockSpec(memory_space=pl.ANY)
    vmem = pl.BlockSpec(memory_space=pltpu.VMEM)
    cells = (SIDE, SIDE, CH)
    block8 = (PEERS, HALF, LANES)
    chunks = (NCH, PEERS, SB, LANES)
    block16 = (PEERS, SIDE, KB)
    per_step = (HALF, LANES, CH)
    heads = (HALF, HID, LANES)
    scratch = [
        (cells, F32), (cells, F32), (per_step, F32), (per_step, F32), (heads, F32), (heads, F32),
        (per_step, BF16),
        ((HID * HALF, LANES), F32),
        (block8, BF16),
        ((2,) + block8, BF16),
        ((COLC, ROW * SIDE, LANES), BF16),
        (block16, BF16),
        (chunks, BF16), (chunks, BF16), (chunks, BF16), (chunks, BF16),
        ((COLC // 2, ROW * SIDE, LANES), BF16),
        (block16, BF16),
        (chunks, F32),
        (chunks, BF16), (chunks, BF16), (chunks, BF16), (chunks, BF16),
        ((2 * HID, CH), BF16),
        ((HID, LANES), F32),
    ]
    update, grad_pair, grad_right = pl.pallas_call(
        kernel,
        out_shape=(pltpu.VMEM(cells, F32), pltpu.VMEM(cells, F32), pltpu.VMEM((HID, SIDE, KB), BF16)),
        in_specs=[any_spec, any_spec, vmem, vmem, vmem, vmem, vmem, any_spec],
        out_specs=(vmem, vmem, vmem),
        scratch_shapes=[pltpu.VMEM(shape, dtype) for shape, dtype in scratch]
        + [
            pltpu.SemaphoreType.DMA((2,)),
            pltpu.SemaphoreType.DMA((4,)),
            pltpu.SemaphoreType.DMA((4,)),
            pltpu.SemaphoreType.DMA((8, NCH)),
            pltpu.SemaphoreType.REGULAR,
        ],
        compiler_params=pltpu.CompilerParams(
            collective_id=0, has_side_effects=True, vmem_limit_bytes=58 * 1024 * 1024
        ),
    )(
        pair,
        jnp.transpose(right_proj, (0, 2, 1)),
        w_left_gate.T,
        w_left.T,
        w_gate,
        out_gain.reshape(1, HID),
        w_out,
        cotangent,
    )
    return update, grad_pair, jnp.transpose(grad_right, (0, 2, 1))


def solution(mesh):
    in_specs = (
        P("row", "col", None),
        P(None, "row", "col"),
        P(),
        P(),
        P(),
        P(),
        P(),
        P("row", "col", None),
    )
    out_specs = (P("row", "col", None), P("row", "col", None), P(None, "row", "col"))
    return jax.shard_map(shards, mesh=mesh, in_specs=in_specs, out_specs=out_specs, check_vma=False)
```

```python
import random

import jax
import jax.numpy as jnp
from jax import lax
from jax.experimental import pallas as pl
from jax.experimental.pallas import tpu as pltpu
from jax.sharding import PartitionSpec as P

EPS = 1e-05
F32 = jnp.float32
BF16 = jnp.bfloat16
MESH = pl.DeviceIdType.MESH

CH = 128
HID = 64
SIDE = 64
ROW = 8
COLC = 8
HALF = SIDE // 2
KB = 128
LANES = 128
PEERS = ROW * COLC
NCH = 2
SB = HALF // NCH
TR = ROW * 2 * SB
UNROLL = 16
STEPS = (0, 1, 2, -1)
OTHERS = [(x, y, z) for x in STEPS for y in STEPS for z in STEPS if (x, y, z) != (0, 0, 0)]
random.Random(1).shuffle(OTHERS)
OTHERS.sort(key=lambda v: -sum(map(abs, v)))
PLANE = [v for v in OTHERS if v[2] == 0]
LINE = [v for v in OTHERS if v[0] == 0 and v[1] == 0]
NEAR = [v for v in OTHERS if v in PLANE or v in LINE]
REST = [v for v in OTHERS if v not in LINE]


def dot(a, b, da, db):
    return lax.dot_general(a, b, (((da,), (db,)), ((), ())), preferred_element_type=F32)


def swap(a, b):
    left = lax.broadcasted_iota(jnp.int32, a.shape, a.ndim - 1) < LANES // 2
    ra = pltpu.roll(a, LANES // 2, a.ndim - 1)
    rb = pltpu.roll(b, LANES // 2, b.ndim - 1)
    return jnp.where(left, a, rb), jnp.where(left, ra, b)


def kernel(
    pair_hbm, right_hbm, wlg_ref, wl_ref, wg_ref, gain_ref, wo_ref, cot_hbm,
    upd, gp, gr,
    raw, xn, cot, inv, gate, sig, val, dgate,
    stage, stage_d, send_l, lb, lfull, rt, tm, tr, dts, dtr, dtfull, grs, dlk, dlx, dly, dls, dlr, wcat, gcol,
    io_sem, send_sem, recv_sem, tri_sem, line_sem,
):
    row, col = lax.axis_index("row"), lax.axis_index("col")
    core = lax.rem(col, 2)
    colc = col // 2
    me = row * COLC + colc
    sibling = (row, colc * 2 + (1 - core))

    across = {d: lax.rem(colc // 2 + d + 4, 4) for d in STEPS}
    up = {d: lax.rem(lax.rem(colc, 2) * 2 + row // 4 + d + 4, 4) for d in STEPS}
    deep = {d: lax.rem(lax.rem(row, 4) + d + 4, 4) for d in STEPS}
    cols = {(x, y): across[x] * 2 + up[y] // 2 for x in STEPS for y in STEPS}
    rows_of = {(y, z): lax.rem(up[y], 2) * 4 + deep[z] for y in STEPS for z in STEPS}

    def peer(v):
        x, y, z = v
        prow, pcol = rows_of[y, z], cols[x, y]
        return prow * COLC + pcol, (prow, pcol * 2 + core)

    load_pair = pltpu.make_async_copy(pair_hbm, raw, io_sem.at[0])
    load_pair.start()
    load_cot = pltpu.make_async_copy(cot_hbm, cot, io_sem.at[1])
    load_cot.start()

    barrier = pltpu.get_barrier_semaphore()
    for v in NEAR:
        pl.semaphore_signal(barrier, inc=1, device_id=peer(v)[1], device_id_type=MESH)
    pl.semaphore_signal(barrier, inc=1, device_id=sibling, device_id_type=MESH)

    def keep(src_of, dst, recv):
        pltpu.make_async_copy(src_of(me), dst, recv).start()

    def exchange(src_of, dst, send, recv, others=OTHERS):
        for v in others:
            q, device = peer(v)
            pltpu.make_async_remote_copy(
                src_ref=src_of(q),
                dst_ref=dst,
                send_sem=send,
                recv_sem=recv,
                device_id=device,
                device_id_type=MESH,
            ).start()

    def arrived(buf, sem):
        pltpu.make_async_copy(buf, buf, sem).wait()

    def sent(buf, sem):
        part = buf.at[pl.ds(0, PEERS - 1)]
        pltpu.make_async_copy(part, part, sem).wait()

    wcat[:HID] = wl_ref[...]
    wcat[HID:] = wlg_ref[...]
    eye = lax.broadcasted_iota(jnp.int32, (HID, HID), 0) == lax.broadcasted_iota(jnp.int32, (HID, HID), 1)
    column = jnp.sum(jnp.where(eye, gain_ref[...], 0.0), axis=1, keepdims=True)
    gcol[...] = jnp.broadcast_to(column, (HID, LANES))

    load_pair.wait()

    def stage_rows(t, n):
        return pl.ds(t * (HID * SB) + n, HID, stride=SB)

    def steps(step, t):
        lax.fori_loop(0, SB, lambda n, _: (step(t, n), 0)[1], 0, unroll=UNROLL)

    def left_step(t, n):
        s = t * SB + n
        x = jnp.concatenate([raw[s], raw[s + HALF]], axis=0)
        centred = x - jnp.mean(x, -1, keepdims=True)
        inv_std = lax.rsqrt(jnp.mean(centred * centred, -1, keepdims=True) + EPS)
        normed = centred * inv_std
        xn[s] = normed[:SIDE]
        xn[s + HALF] = normed[SIDE:]
        inv[s] = jnp.broadcast_to(inv_std, (LANES, CH))
        both = dot(wcat[...], normed.astype(BF16), 1, 1)
        value = both[:HID]
        left_sig = jax.nn.sigmoid(both[HID:])
        val[s] = value
        sig[s] = left_sig
        stage[stage_rows(t, n), :] = left_sig * value

    steps(left_step, 0)
    pl.semaphore_wait(barrier, len(NEAR) + 1)
    exchange(lambda q: right_hbm.at[q], rt.at[me], send_sem.at[0], line_sem, LINE)
    steps(left_step, 1)

    def stage_block(t, h):
        return pl.ds(pl.multiple_of((t * HID + h) * SB, SB), SB)

    def pack_left(h, _):
        send_l[h] = jnp.concatenate([stage[stage_block(t, h), :] for t in range(NCH)], axis=0).astype(BF16)
        return 0

    lax.fori_loop(0, HID, pack_left, 0, unroll=4)
    arrived(rt.at[pl.ds(0, len(LINE))], line_sem)
    keep(lambda q: send_l.at[q], lb.at[core, me], recv_sem.at[1])
    exchange(lambda q: send_l.at[q], lb.at[core, me], send_sem.at[1], recv_sem.at[1])
    keep(lambda q: right_hbm.at[q], rt.at[me], recv_sem.at[0])
    exchange(lambda q: right_hbm.at[q], rt.at[me], send_sem.at[0], recv_sem.at[0], REST)

    def gate_step(s, _):
        low = jnp.concatenate([xn[s], xn[s + HALF]], axis=0).astype(BF16)
        gate[s] = jax.nn.sigmoid(dot(low, wg_ref[...], 1, 0))
        return 0

    lax.fori_loop(0, HALF, gate_step, 0, unroll=UNROLL)

    arrived(lb.at[core], recv_sem.at[1])
    swap_left = pltpu.make_async_remote_copy(
        src_ref=lb.at[core],
        dst_ref=lb.at[core],
        send_sem=send_sem.at[2],
        recv_sem=recv_sem.at[2],
        device_id=sibling,
        device_id_type=MESH,
    )
    swap_left.start()
    arrived(lb.at[1 - core], recv_sem.at[2])

    def unpack_left(q, _):
        r, c = q // COLC, lax.rem(q, COLC)
        top, bottom = swap(lb[0, q].astype(F32), lb[1, q].astype(F32))
        for t in range(NCH):
            block = jnp.concatenate([top[t * SB : (t + 1) * SB], bottom[t * SB : (t + 1) * SB]], axis=0)
            at = pl.multiple_of(t * TR + r * 2 * SB, 2 * SB)
            lfull[c, pl.ds(at, 2 * SB), :] = block.astype(BF16)
        return 0

    lax.fori_loop(0, PEERS, unpack_left, 0, unroll=4)

    def k_left(lo, rows=slice(None)):
        return jnp.concatenate([lfull[lo, rows], lfull[lo + 1, rows]], axis=1)

    def k_right(lo):
        a = jnp.concatenate([rt[lo * COLC + c] for c in range(COLC)], axis=0)
        b = jnp.concatenate([rt[(lo + 1) * COLC + c] for c in range(COLC)], axis=0)
        return jnp.concatenate([a, b], axis=1)

    arrived(rt.at[pl.ds(0, PEERS - len(LINE))], recv_sem.at[0])

    for t in range(NCH):
        rows = slice(t * TR, (t + 1) * TR)
        total = dot(k_left(0, rows), k_right(0), 1, 1)
        for lo in range(2, ROW, 2):
            total += dot(k_left(lo, rows), k_right(lo), 1, 1)
        for r in range(ROW):
            for p in range(COLC // 2):
                lanes = slice(p * LANES, (p + 1) * LANES)
                a, b = swap(
                    total[r * 2 * SB : r * 2 * SB + SB, lanes],
                    total[r * 2 * SB + SB : (r + 1) * 2 * SB, lanes],
                )
                tm[t, r * COLC + 2 * p] = a.astype(BF16)
                tm[t, r * COLC + 2 * p + 1] = b.astype(BF16)
        if t:
            sent(tm.at[t - 1], tri_sem.at[0, t - 1])
        keep(lambda q: tm.at[t, q], tr.at[t, me], tri_sem.at[1, t])
        exchange(lambda q: tm.at[t, q], tr.at[t, me], tri_sem.at[0, t], tri_sem.at[1, t])

    def widen(buf, t):
        def one(h, _):
            stage[stage_block(t, h), :] = buf[t, h].astype(F32)
            return 0

        lax.fori_loop(0, HID, one, 0, unroll=8)

    def middle_step(t, n):
        s = t * SB + n
        tri = stage[stage_rows(t, n), :]
        centred = tri - jnp.mean(tri, 0, keepdims=True)
        inv_out = lax.rsqrt(jnp.mean(centred * centred, 0, keepdims=True) + EPS)
        hat = centred * inv_out
        gain = gcol[...]
        linear = dot((hat * gain).astype(BF16), wo_ref[...], 0, 0)
        g = gate[s]
        update = g * linear
        upd[s] = update[:SIDE]
        upd[s + HALF] = update[SIDE:]
        ct = jnp.concatenate([cot[s], cot[s + HALF]], axis=0)
        d_linear = ct * g
        dgate[s] = (ct * linear * g * (1.0 - g)).astype(BF16)
        d_scaled = dot(wo_ref[...], d_linear.astype(BF16), 1, 1) * gain
        d_tri = inv_out * (
            d_scaled
            - jnp.mean(d_scaled, 0, keepdims=True)
            - hat * jnp.mean(d_scaled * hat, 0, keepdims=True)
        )
        stage_d[stage_rows(t, n), :] = d_tri

    load_cot.wait()
    for t in range(NCH):
        arrived(tr.at[t], tri_sem.at[1, t])
        widen(tr, t)
        steps(middle_step, t)

        def pack_tri(h, _):
            dts[t, h] = stage_d[stage_block(t, h), :].astype(BF16)
            return 0

        lax.fori_loop(0, HID, pack_tri, 0, unroll=8)
        keep(lambda q: dts.at[t, q], dtr.at[t, me], tri_sem.at[3, t])
        exchange(lambda q: dts.at[t, q], dtr.at[t, me], tri_sem.at[2, t], tri_sem.at[3, t])

    def swap_grad(t):
        return pltpu.make_async_remote_copy(
            src_ref=dlx.at[t],
            dst_ref=dly.at[t],
            send_sem=tri_sem.at[4, t],
            recv_sem=tri_sem.at[5, t],
            device_id=sibling,
            device_id_type=MESH,
        )

    def tri_grad(t):
        arrived(dtr.at[t], tri_sem.at[3, t])

        def unpack_tri(n, _):
            r, p = n // (COLC // 2), lax.rem(n, COLC // 2)
            at = r * COLC + 2 * p
            top, bottom = swap(dtr[t, at].astype(F32), dtr[t, at + 1].astype(F32))
            block = jnp.concatenate([top, bottom], axis=0).astype(BF16)
            dtfull[p, pl.ds(pl.multiple_of(t * TR + r * 2 * SB, 2 * SB), 2 * SB), :] = block
            return 0

        lax.fori_loop(0, PEERS // 2, unpack_tri, 0, unroll=8)

    def left_grad(t):
        d_tri = jnp.concatenate([dtfull[p, t * TR : (t + 1) * TR] for p in range(COLC // 2)], axis=1)
        for lo in range(0, ROW, 2):
            part = dot(d_tri, k_right(lo), 1, 0)
            for c in range(2):
                for r in range(ROW):
                    lanes = slice(c * LANES, (c + 1) * LANES)
                    for_0, for_1 = swap(
                        part[r * 2 * SB : r * 2 * SB + SB, lanes],
                        part[r * 2 * SB + SB : (r + 1) * 2 * SB, lanes],
                    )
                    at = r * COLC + lo + c
                    first = core == 0
                    dlk[t, at] = jnp.where(first, for_0, for_1)
                    dlx[t, at] = jnp.where(first, for_1, for_0).astype(BF16)
        swap_grad(t).start()

    def send_left_grad(t):
        swap_grad(t).wait_recv()

        def add_halves(q, _):
            dls[t, q] = (dlk[t, q] + dly[t, q].astype(F32)).astype(BF16)
            return 0

        lax.fori_loop(0, PEERS, add_halves, 0, unroll=8)
        keep(lambda q: dls.at[t, q], dlr.at[t, me], tri_sem.at[7, t])
        exchange(lambda q: dls.at[t, q], dlr.at[t, me], tri_sem.at[6, t], tri_sem.at[7, t])

    for t in range(NCH - 1):
        tri_grad(t)
        left_grad(t)
        send_left_grad(t)
    tri_grad(NCH - 1)

    d_tri_all = jnp.concatenate([dtfull[p] for p in range(COLC // 2)], axis=1)
    for lo in range(0, COLC, 2):
        part = dot(d_tri_all, k_left(lo), 0, 0).astype(BF16)
        for c in range(2):
            for cc in range(COLC):
                grs[(lo + c) * COLC + cc] = part[cc * SIDE : (cc + 1) * SIDE, c * LANES : (c + 1) * LANES]

    def send_right_grad(others):
        exchange(lambda q: grs.at[q], gr.at[me], send_sem.at[3], recv_sem.at[3], others)

    keep(lambda q: grs.at[q], gr.at[me], recv_sem.at[3])
    send_right_grad(OTHERS[0::4])
    left_grad(NCH - 1)
    send_left_grad(NCH - 1)
    send_right_grad([v for n, v in enumerate(OTHERS) if n % 4])

    def final_step(t, n):
        s = t * SB + n
        d_left = stage[stage_rows(t, n), :]
        left_sig, value = sig[s], val[s]
        d_value = d_left * left_sig
        d_logit = d_left * value * left_sig * (1.0 - left_sig)
        stacked = jnp.concatenate([d_value, d_logit], axis=0).astype(BF16)
        grad = dot(stacked, wcat[...], 0, 0) + dot(dgate[s], wg_ref[...], 1, 1)
        normed = jnp.concatenate([xn[s], xn[s + HALF]], axis=0)
        out = inv[s] * (
            grad
            - jnp.mean(grad, -1, keepdims=True)
            - normed * jnp.mean(grad * normed, -1, keepdims=True)
        )
        gp[s] = out[:SIDE]
        gp[s + HALF] = out[SIDE:]

    for t in range(NCH):
        arrived(dlr.at[t], tri_sem.at[7, t])
        widen(dlr, t)
        steps(final_step, t)

    sent(right_hbm, send_sem.at[0])
    sent(send_l, send_sem.at[1])
    swap_left.wait_send()
    for t in range(NCH):
        sent(dts.at[t], tri_sem.at[2, t])
        swap_grad(t).wait_send()
    sent(tm.at[NCH - 1], tri_sem.at[0, NCH - 1])
    for t in range(NCH):
        sent(dls.at[t], tri_sem.at[6, t])
    sent(grs, send_sem.at[3])
    arrived(gr, recv_sem.at[3])


def store(upd, gp, gr, upd_out, gp_out, gr_out, sem):
    copies = [
        pltpu.make_async_copy(src, dst, sem.at[n])
        for n, (src, dst) in enumerate(((upd, upd_out), (gp, gp_out), (gr, gr_out)))
    ]
    for copy in copies:
        copy.start()
    for copy in copies:
        copy.wait()


def shards(pair, right_proj, w_left_gate, w_left, w_gate, out_gain, w_out, cotangent):
    any_spec = pl.BlockSpec(memory_space=pl.ANY)
    vmem = pl.BlockSpec(memory_space=pltpu.VMEM)
    cells = (SIDE, SIDE, CH)
    block8 = (PEERS, HALF, LANES)
    chunks = (NCH, PEERS, SB, LANES)
    block16 = (PEERS, SIDE, KB)
    per_step = (HALF, LANES, CH)
    heads = (HALF, HID, LANES)
    scratch = [
        (cells, F32), (cells, F32), (cells, F32), (per_step, F32), (per_step, F32), (heads, F32), (heads, F32),
        (per_step, BF16),
        ((HID * HALF, LANES), F32), ((HID * HALF, LANES), F32),
        (block8, BF16),
        ((2,) + block8, BF16),
        ((COLC, ROW * SIDE, LANES), BF16),
        (block16, BF16),
        (chunks, BF16), (chunks, BF16), (chunks, BF16), (chunks, BF16),
        ((COLC // 2, ROW * SIDE, LANES), BF16),
        (block16, BF16),
        (chunks, F32),
        (chunks, BF16), (chunks, BF16), (chunks, BF16), (chunks, BF16),
        ((2 * HID, CH), BF16),
        ((HID, LANES), F32),
    ]
    update, grad_pair, grad_right = pl.pallas_call(
        kernel,
        out_shape=(pltpu.VMEM(cells, F32), pltpu.VMEM(cells, F32), pltpu.VMEM((HID, SIDE, KB), BF16)),
        in_specs=[any_spec, any_spec, vmem, vmem, vmem, vmem, vmem, any_spec],
        out_specs=(vmem, vmem, vmem),
        scratch_shapes=[pltpu.VMEM(shape, dtype) for shape, dtype in scratch]
        + [
            pltpu.SemaphoreType.DMA((2,)),
            pltpu.SemaphoreType.DMA((4,)),
            pltpu.SemaphoreType.DMA((4,)),
            pltpu.SemaphoreType.DMA((8, NCH)),
            pltpu.SemaphoreType.DMA,
        ],
        compiler_params=pltpu.CompilerParams(
            collective_id=0, has_side_effects=True, vmem_limit_bytes=58 * 1024 * 1024
        ),
    )(
        pair,
        jnp.transpose(right_proj, (0, 2, 1)),
        w_left_gate.T,
        w_left.T,
        w_gate,
        out_gain.reshape(1, HID),
        w_out,
        cotangent,
    )
    update, grad_pair, grad_right = pl.pallas_call(
        store,
        out_shape=(
            jax.ShapeDtypeStruct(cells, F32),
            jax.ShapeDtypeStruct(cells, F32),
            jax.ShapeDtypeStruct((HID, SIDE, KB), BF16),
        ),
        in_specs=[vmem, vmem, vmem],
        out_specs=(any_spec, any_spec, any_spec),
        scratch_shapes=[pltpu.SemaphoreType.DMA((3,))],
        compiler_params=pltpu.CompilerParams(vmem_limit_bytes=1024 * 1024),
    )(*(pltpu.with_memory_space_constraint(a, pltpu.VMEM) for a in (update, grad_pair, grad_right)))
    return update, grad_pair, jnp.transpose(grad_right, (0, 2, 1))


def solution(mesh):
    in_specs = (
        P("row", "col", None),
        P(None, "row", "col"),
        P(),
        P(),
        P(),
        P(),
        P(),
        P("row", "col", None),
    )
    out_specs = (P("row", "col", None), P("row", "col", None), P(None, "row", "col"))
    return jax.shard_map(shards, mesh=mesh, in_specs=in_specs, out_specs=out_specs, check_vma=False)
```

```python
import random

import jax
import jax.numpy as jnp
from jax import lax
from jax.experimental import pallas as pl
from jax.experimental.pallas import tpu as pltpu
from jax.sharding import PartitionSpec as P

EPS = 1e-05
F32 = jnp.float32
BF16 = jnp.bfloat16
MESH = pl.DeviceIdType.MESH

CH = 128
HID = 64
SIDE = 64
ROW = 8
COLC = 8
HALF = SIDE // 2
KB = 128
LANES = 128
PEERS = ROW * COLC
NCH = 2
SB = HALF // NCH
TR = ROW * 2 * SB
UNROLL = 16
STEPS = (0, 1, 2, -1)
OTHERS = [(x, y, z) for x in STEPS for y in STEPS for z in STEPS if (x, y, z) != (0, 0, 0)]
random.Random(1).shuffle(OTHERS)
OTHERS.sort(key=lambda v: -sum(map(abs, v)))
PLANE = [v for v in OTHERS if v[2] == 0]
LINE = [v for v in OTHERS if v[0] == 0 and v[1] == 0]
NEAR = [v for v in OTHERS if v in PLANE or v in LINE]
REST = [v for v in OTHERS if v not in LINE]


def dot(a, b, da, db):
    return lax.dot_general(a, b, (((da,), (db,)), ((), ())), preferred_element_type=F32)


def swap(a, b):
    left = lax.broadcasted_iota(jnp.int32, a.shape, a.ndim - 1) < LANES // 2
    ra = pltpu.roll(a, LANES // 2, a.ndim - 1)
    rb = pltpu.roll(b, LANES // 2, b.ndim - 1)
    return jnp.where(left, a, rb), jnp.where(left, ra, b)


def kernel(
    pair_hbm, right_hbm, wlg_ref, wl_ref, wg_ref, gain_ref, wo_ref, cot_hbm,
    upd, gp, gr,
    raw, xn, cot, inv, gate, sig, val, dgate,
    stage, stage_d, send_l, lb, lfull, rt, tm, tr, dts, dtr, dtfull, grsum, grs, dlk, dlx, dly, dls, dlr, wcat, gcol,
    io_sem, send_sem, recv_sem, tri_sem, line_sem,
):
    row, col = lax.axis_index("row"), lax.axis_index("col")
    core = lax.rem(col, 2)
    colc = col // 2
    me = row * COLC + colc
    sibling = (row, colc * 2 + (1 - core))

    across = {d: lax.rem(colc // 2 + d + 4, 4) for d in STEPS}
    up = {d: lax.rem(lax.rem(colc, 2) * 2 + row // 4 + d + 4, 4) for d in STEPS}
    deep = {d: lax.rem(lax.rem(row, 4) + d + 4, 4) for d in STEPS}
    cols = {(x, y): across[x] * 2 + up[y] // 2 for x in STEPS for y in STEPS}
    rows_of = {(y, z): lax.rem(up[y], 2) * 4 + deep[z] for y in STEPS for z in STEPS}

    def peer(v):
        x, y, z = v
        prow, pcol = rows_of[y, z], cols[x, y]
        return prow * COLC + pcol, (prow, pcol * 2 + core)

    load_pair = pltpu.make_async_copy(pair_hbm, raw, io_sem.at[0])
    load_pair.start()
    load_cot = pltpu.make_async_copy(cot_hbm, cot, io_sem.at[1])
    load_cot.start()

    barrier = pltpu.get_barrier_semaphore()
    for v in NEAR:
        pl.semaphore_signal(barrier, inc=1, device_id=peer(v)[1], device_id_type=MESH)
    pl.semaphore_signal(barrier, inc=1, device_id=sibling, device_id_type=MESH)

    def keep(src_of, dst, recv):
        pltpu.make_async_copy(src_of(me), dst, recv).start()

    def exchange(src_of, dst, send, recv, others=OTHERS):
        for v in others:
            q, device = peer(v)
            pltpu.make_async_remote_copy(
                src_ref=src_of(q),
                dst_ref=dst,
                send_sem=send,
                recv_sem=recv,
                device_id=device,
                device_id_type=MESH,
            ).start()

    def arrived(buf, sem):
        pltpu.make_async_copy(buf, buf, sem).wait()

    def sent(buf, sem):
        part = buf.at[pl.ds(0, PEERS - 1)]
        pltpu.make_async_copy(part, part, sem).wait()

    wcat[:HID] = wl_ref[...]
    wcat[HID:] = wlg_ref[...]
    eye = lax.broadcasted_iota(jnp.int32, (HID, HID), 0) == lax.broadcasted_iota(jnp.int32, (HID, HID), 1)
    column = jnp.sum(jnp.where(eye, gain_ref[...], 0.0), axis=1, keepdims=True)
    gcol[...] = jnp.broadcast_to(column, (HID, LANES))

    load_pair.wait()

    def stage_rows(t, n):
        return pl.ds(t * (HID * SB) + n, HID, stride=SB)

    def steps(step, t):
        lax.fori_loop(0, SB, lambda n, _: (step(t, n), 0)[1], 0, unroll=UNROLL)

    def left_step(t, n):
        s = t * SB + n
        x = jnp.concatenate([raw[s], raw[s + HALF]], axis=0)
        centred = x - jnp.mean(x, -1, keepdims=True)
        inv_std = lax.rsqrt(jnp.mean(centred * centred, -1, keepdims=True) + EPS)
        normed = centred * inv_std
        xn[s] = normed[:SIDE]
        xn[s + HALF] = normed[SIDE:]
        inv[s] = jnp.broadcast_to(inv_std, (LANES, CH))
        both = dot(wcat[...], normed.astype(BF16), 1, 1)
        value = both[:HID]
        left_sig = jax.nn.sigmoid(both[HID:])
        val[s] = value
        sig[s] = left_sig
        stage[stage_rows(t, n), :] = left_sig * value

    def stage_block(t, h):
        return pl.ds(pl.multiple_of((t * HID + h) * SB, SB), SB)

    def project_left(t):
        steps(left_step, t)

        def pack_left(h, _):
            send_l[t, h] = stage[stage_block(t, h), :].astype(BF16)
            return 0

        lax.fori_loop(0, HID, pack_left, 0, unroll=8)

    def send_left(t):
        keep(lambda q: send_l.at[t, q], lb.at[t, core, me], tri_sem.at[9, t])
        exchange(lambda q: send_l.at[t, q], lb.at[t, core, me], tri_sem.at[8, t], tri_sem.at[9, t])

    project_left(0)
    pl.semaphore_wait(barrier, len(NEAR) + 1)
    exchange(lambda q: right_hbm.at[q], rt.at[me], send_sem.at[0], line_sem, LINE)
    keep(lambda q: right_hbm.at[q], rt.at[me], recv_sem.at[0])
    project_left(1)
    arrived(rt.at[pl.ds(0, len(LINE))], line_sem)
    send_left(0)
    exchange(lambda q: right_hbm.at[q], rt.at[me], send_sem.at[0], recv_sem.at[0], REST)

    def gate_step(s, _):
        low = jnp.concatenate([xn[s], xn[s + HALF]], axis=0).astype(BF16)
        gate[s] = jax.nn.sigmoid(dot(low, wg_ref[...], 1, 0))
        return 0

    lax.fori_loop(0, HALF, gate_step, 0, unroll=UNROLL)

    def swap_left(t):
        return pltpu.make_async_remote_copy(
            src_ref=lb.at[t, core],
            dst_ref=lb.at[t, core],
            send_sem=tri_sem.at[10, t],
            recv_sem=tri_sem.at[11, t],
            device_id=sibling,
            device_id_type=MESH,
        )

    def take_left(t):
        arrived(lb.at[t, core], tri_sem.at[9, t])
        swap_left(t).start()
        arrived(lb.at[t, 1 - core], tri_sem.at[11, t])

        def unpack_left(q, _):
            r, c = q // COLC, lax.rem(q, COLC)
            top, bottom = swap(lb[t, 0, q].astype(F32), lb[t, 1, q].astype(F32))
            block = jnp.concatenate([top, bottom], axis=0).astype(BF16)
            lfull[c, pl.ds(pl.multiple_of(t * TR + r * 2 * SB, 2 * SB), 2 * SB), :] = block
            return 0

        lax.fori_loop(0, PEERS, unpack_left, 0, unroll=8)

    def k_left(lo, rows=slice(None)):
        return jnp.concatenate([lfull[lo, rows], lfull[lo + 1, rows]], axis=1)

    def k_right(lo):
        a = jnp.concatenate([rt[lo * COLC + c] for c in range(COLC)], axis=0)
        b = jnp.concatenate([rt[(lo + 1) * COLC + c] for c in range(COLC)], axis=0)
        return jnp.concatenate([a, b], axis=1)

    send_left(1)
    take_left(0)
    sent(right_hbm, send_sem.at[0])
    arrived(rt.at[pl.ds(0, PEERS - len(LINE))], recv_sem.at[0])

    for t in range(NCH):
        if t:
            take_left(t)
        rows = slice(t * TR, (t + 1) * TR)
        total = dot(k_left(0, rows), k_right(0), 1, 1)
        for lo in range(2, ROW, 2):
            total += dot(k_left(lo, rows), k_right(lo), 1, 1)
        for r in range(ROW):
            for p in range(COLC // 2):
                lanes = slice(p * LANES, (p + 1) * LANES)
                a, b = swap(
                    total[r * 2 * SB : r * 2 * SB + SB, lanes],
                    total[r * 2 * SB + SB : (r + 1) * 2 * SB, lanes],
                )
                tm[t, r * COLC + 2 * p] = a.astype(BF16)
                tm[t, r * COLC + 2 * p + 1] = b.astype(BF16)
        if t:
            sent(tm.at[t - 1], tri_sem.at[0, t - 1])
        keep(lambda q: tm.at[t, q], tr.at[t, me], tri_sem.at[1, t])
        exchange(lambda q: tm.at[t, q], tr.at[t, me], tri_sem.at[0, t], tri_sem.at[1, t])

    def widen(buf, t):
        def one(h, _):
            stage[stage_block(t, h), :] = buf[t, h].astype(F32)
            return 0

        lax.fori_loop(0, HID, one, 0, unroll=8)

    def middle_step(t, n):
        s = t * SB + n
        tri = stage[stage_rows(t, n), :]
        centred = tri - jnp.mean(tri, 0, keepdims=True)
        inv_out = lax.rsqrt(jnp.mean(centred * centred, 0, keepdims=True) + EPS)
        hat = centred * inv_out
        gain = gcol[...]
        linear = dot((hat * gain).astype(BF16), wo_ref[...], 0, 0)
        g = gate[s]
        update = g * linear
        upd[s] = update[:SIDE]
        upd[s + HALF] = update[SIDE:]
        ct = jnp.concatenate([cot[s], cot[s + HALF]], axis=0)
        d_linear = ct * g
        dgate[s] = (ct * linear * g * (1.0 - g)).astype(BF16)
        d_scaled = dot(wo_ref[...], d_linear.astype(BF16), 1, 1) * gain
        d_tri = inv_out * (
            d_scaled
            - jnp.mean(d_scaled, 0, keepdims=True)
            - hat * jnp.mean(d_scaled * hat, 0, keepdims=True)
        )
        stage_d[stage_rows(t, n), :] = d_tri

    load_cot.wait()
    for t in range(NCH):
        arrived(tr.at[t], tri_sem.at[1, t])
        widen(tr, t)
        steps(middle_step, t)

        def pack_tri(h, _):
            dts[t, h] = stage_d[stage_block(t, h), :].astype(BF16)
            return 0

        lax.fori_loop(0, HID, pack_tri, 0, unroll=8)
        keep(lambda q: dts.at[t, q], dtr.at[t, me], tri_sem.at[3, t])
        exchange(lambda q: dts.at[t, q], dtr.at[t, me], tri_sem.at[2, t], tri_sem.at[3, t])

    def swap_grad(t):
        return pltpu.make_async_remote_copy(
            src_ref=dlx.at[t],
            dst_ref=dly.at[t],
            send_sem=tri_sem.at[4, t],
            recv_sem=tri_sem.at[5, t],
            device_id=sibling,
            device_id_type=MESH,
        )

    def tri_grad(t):
        arrived(dtr.at[t], tri_sem.at[3, t])

        def unpack_tri(n, _):
            r, p = n // (COLC // 2), lax.rem(n, COLC // 2)
            at = r * COLC + 2 * p
            top, bottom = swap(dtr[t, at].astype(F32), dtr[t, at + 1].astype(F32))
            block = jnp.concatenate([top, bottom], axis=0).astype(BF16)
            dtfull[p, pl.ds(pl.multiple_of(t * TR + r * 2 * SB, 2 * SB), 2 * SB), :] = block
            return 0

        lax.fori_loop(0, PEERS // 2, unpack_tri, 0, unroll=8)

    def left_grad(t):
        d_tri = jnp.concatenate([dtfull[p, t * TR : (t + 1) * TR] for p in range(COLC // 2)], axis=1)
        for lo in range(0, ROW, 2):
            part = dot(d_tri, k_right(lo), 1, 0)
            for c in range(2):
                for r in range(ROW):
                    lanes = slice(c * LANES, (c + 1) * LANES)
                    for_0, for_1 = swap(
                        part[r * 2 * SB : r * 2 * SB + SB, lanes],
                        part[r * 2 * SB + SB : (r + 1) * 2 * SB, lanes],
                    )
                    at = r * COLC + lo + c
                    first = core == 0
                    dlk[t, at] = jnp.where(first, for_0, for_1)
                    dlx[t, at] = jnp.where(first, for_1, for_0).astype(BF16)
        swap_grad(t).start()

    def send_left_grad(t):
        swap_grad(t).wait_recv()

        def add_halves(q, _):
            dls[t, q] = (dlk[t, q] + dly[t, q].astype(F32)).astype(BF16)
            return 0

        lax.fori_loop(0, PEERS, add_halves, 0, unroll=8)
        keep(lambda q: dls.at[t, q], dlr.at[t, me], tri_sem.at[7, t])
        exchange(lambda q: dls.at[t, q], dlr.at[t, me], tri_sem.at[6, t], tri_sem.at[7, t])

    def right_grad(t):
        rows = slice(t * TR, (t + 1) * TR)
        d_tri = jnp.concatenate([dtfull[p, rows] for p in range(COLC // 2)], axis=1)
        for lo in range(0, COLC, 2):
            part = dot(d_tri, k_left(lo, rows), 0, 0)
            if t:
                part += grsum[lo // 2]
            if t < NCH - 1:
                grsum[lo // 2] = part
                continue
            part = part.astype(BF16)
            for c in range(2):
                for cc in range(COLC):
                    grs[(lo + c) * COLC + cc] = part[cc * SIDE : (cc + 1) * SIDE, c * LANES : (c + 1) * LANES]

    for t in range(NCH - 1):
        tri_grad(t)
        left_grad(t)
        right_grad(t)
        send_left_grad(t)
    tri_grad(NCH - 1)

    right_grad(NCH - 1)

    def send_right_grad(others):
        exchange(lambda q: grs.at[q], gr.at[me], send_sem.at[3], recv_sem.at[3], others)

    keep(lambda q: grs.at[q], gr.at[me], recv_sem.at[3])
    send_right_grad(OTHERS[0::4])
    left_grad(NCH - 1)
    send_left_grad(NCH - 1)
    send_right_grad([v for n, v in enumerate(OTHERS) if n % 4])

    def final_step(t, n):
        s = t * SB + n
        d_left = stage[stage_rows(t, n), :]
        left_sig, value = sig[s], val[s]
        d_value = d_left * left_sig
        d_logit = d_left * value * left_sig * (1.0 - left_sig)
        stacked = jnp.concatenate([d_value, d_logit], axis=0).astype(BF16)
        grad = dot(stacked, wcat[...], 0, 0) + dot(dgate[s], wg_ref[...], 1, 1)
        normed = jnp.concatenate([xn[s], xn[s + HALF]], axis=0)
        out = inv[s] * (
            grad
            - jnp.mean(grad, -1, keepdims=True)
            - normed * jnp.mean(grad * normed, -1, keepdims=True)
        )
        gp[s] = out[:SIDE]
        gp[s + HALF] = out[SIDE:]

    for t in range(NCH):
        arrived(dlr.at[t], tri_sem.at[7, t])
        widen(dlr, t)
        steps(final_step, t)

    for t in range(NCH):
        sent(dts.at[t], tri_sem.at[2, t])
        swap_grad(t).wait_send()
        sent(send_l.at[t], tri_sem.at[8, t])
        swap_left(t).wait_send()
    sent(tm.at[NCH - 1], tri_sem.at[0, NCH - 1])
    for t in range(NCH):
        sent(dls.at[t], tri_sem.at[6, t])
    sent(grs, send_sem.at[3])
    arrived(gr, recv_sem.at[3])


def store(upd, gp, gr, upd_out, gp_out, gr_out, sem):
    copies = [
        pltpu.make_async_copy(src, dst, sem.at[n])
        for n, (src, dst) in enumerate(((upd, upd_out), (gp, gp_out), (gr, gr_out)))
    ]
    for copy in copies:
        copy.start()
    for copy in copies:
        copy.wait()


def shards(pair, right_proj, w_left_gate, w_left, w_gate, out_gain, w_out, cotangent):
    any_spec = pl.BlockSpec(memory_space=pl.ANY)
    vmem = pl.BlockSpec(memory_space=pltpu.VMEM)
    cells = (SIDE, SIDE, CH)
    chunks = (NCH, PEERS, SB, LANES)
    block16 = (PEERS, SIDE, KB)
    per_step = (HALF, LANES, CH)
    heads = (HALF, HID, LANES)
    scratch = [
        (cells, F32), (cells, F32), (cells, F32), (per_step, F32), (per_step, F32), (heads, F32), (heads, F32),
        (per_step, BF16),
        ((HID * HALF, LANES), F32), ((HID * HALF, LANES), F32),
        (chunks, BF16),
        ((NCH, 2, PEERS, SB, LANES), BF16),
        ((COLC, ROW * SIDE, LANES), BF16),
        (block16, BF16),
        (chunks, BF16), (chunks, BF16), (chunks, BF16), (chunks, BF16),
        ((COLC // 2, ROW * SIDE, LANES), BF16),
        ((COLC // 2, COLC * SIDE, 2 * LANES), F32),
        (block16, BF16),
        (chunks, F32),
        (chunks, BF16), (chunks, BF16), (chunks, BF16), (chunks, BF16),
        ((2 * HID, CH), BF16),
        ((HID, LANES), F32),
    ]
    update, grad_pair, grad_right = pl.pallas_call(
        kernel,
        out_shape=(pltpu.VMEM(cells, F32), pltpu.VMEM(cells, F32), pltpu.VMEM((HID, SIDE, KB), BF16)),
        in_specs=[any_spec, any_spec, vmem, vmem, vmem, vmem, vmem, any_spec],
        out_specs=(vmem, vmem, vmem),
        scratch_shapes=[pltpu.VMEM(shape, dtype) for shape, dtype in scratch]
        + [
            pltpu.SemaphoreType.DMA((2,)),
            pltpu.SemaphoreType.DMA((4,)),
            pltpu.SemaphoreType.DMA((4,)),
            pltpu.SemaphoreType.DMA((12, NCH)),
            pltpu.SemaphoreType.DMA,
        ],
        compiler_params=pltpu.CompilerParams(
            collective_id=0, has_side_effects=True, vmem_limit_bytes=58 * 1024 * 1024
        ),
    )(
        pair,
        jnp.transpose(right_proj, (0, 2, 1)),
        w_left_gate.T,
        w_left.T,
        w_gate,
        out_gain.reshape(1, HID),
        w_out,
        cotangent,
    )
    update, grad_pair, grad_right = pl.pallas_call(
        store,
        out_shape=(
            jax.ShapeDtypeStruct(cells, F32),
            jax.ShapeDtypeStruct(cells, F32),
            jax.ShapeDtypeStruct((HID, SIDE, KB), BF16),
        ),
        in_specs=[vmem, vmem, vmem],
        out_specs=(any_spec, any_spec, any_spec),
        scratch_shapes=[pltpu.SemaphoreType.DMA((3,))],
        compiler_params=pltpu.CompilerParams(vmem_limit_bytes=1024 * 1024),
    )(*(pltpu.with_memory_space_constraint(a, pltpu.VMEM) for a in (update, grad_pair, grad_right)))
    return update, grad_pair, jnp.transpose(grad_right, (0, 2, 1))


def solution(mesh):
    in_specs = (
        P("row", "col", None),
        P(None, "row", "col"),
        P(),
        P(),
        P(),
        P(),
        P(),
        P("row", "col", None),
    )
    out_specs = (P("row", "col", None), P("row", "col", None), P(None, "row", "col"))
    return jax.shard_map(shards, mesh=mesh, in_specs=in_specs, out_specs=out_specs, check_vma=False)
```

```python
import random

import jax
import jax.numpy as jnp
from jax import lax
from jax.experimental import pallas as pl
from jax.experimental.pallas import tpu as pltpu
from jax.sharding import PartitionSpec as P

EPS = 1e-05
F32 = jnp.float32
BF16 = jnp.bfloat16
MESH = pl.DeviceIdType.MESH

CH = 128
HID = 64
SIDE = 64
ROW = 8
COLC = 8
HALF = SIDE // 2
KB = 128
LANES = 128
PEERS = ROW * COLC
NCH = 2
SB = HALF // NCH
TR = ROW * 2 * SB
UNROLL = 16
STEPS = (0, 1, 2, -1)
OTHERS = [(x, y, z) for x in STEPS for y in STEPS for z in STEPS if (x, y, z) != (0, 0, 0)]
random.Random(1).shuffle(OTHERS)
OTHERS.sort(key=lambda v: -sum(map(abs, v)))
PLANE = [v for v in OTHERS if v[2] == 0]
LINE = [v for v in OTHERS if v[0] == 0 and v[1] == 0]
NEAR = [v for v in OTHERS if v in PLANE or v in LINE]
REST = [v for v in OTHERS if v not in LINE]


def dot(a, b, da, db):
    return lax.dot_general(a, b, (((da,), (db,)), ((), ())), preferred_element_type=F32)


def swap(a, b):
    left = lax.broadcasted_iota(jnp.int32, a.shape, a.ndim - 1) < LANES // 2
    ra = pltpu.roll(a, LANES // 2, a.ndim - 1)
    rb = pltpu.roll(b, LANES // 2, b.ndim - 1)
    return jnp.where(left, a, rb), jnp.where(left, ra, b)


def kernel(
    pair_hbm, right_hbm, wlg_ref, wl_ref, wg_ref, gain_ref, wo_ref, cot_hbm,
    upd, gp, gr,
    raw, xn, cot, inv, gate, sig, val, dgate,
    stage, stage_d, send_l, lb, lfull, rt, tm, tr, dts, dtr, dtfull, grsum, grs, dlk, dlx, dly, dls, dlr, wcat, gcol,
    io_sem, send_sem, recv_sem, tri_sem, line_sem,
):
    row, col = lax.axis_index("row"), lax.axis_index("col")
    core = lax.rem(col, 2)
    colc = col // 2
    me = row * COLC + colc
    sibling = (row, colc * 2 + (1 - core))

    across = {d: lax.rem(colc // 2 + d + 4, 4) for d in STEPS}
    up = {d: lax.rem(lax.rem(colc, 2) * 2 + row // 4 + d + 4, 4) for d in STEPS}
    deep = {d: lax.rem(lax.rem(row, 4) + d + 4, 4) for d in STEPS}
    cols = {(x, y): across[x] * 2 + up[y] // 2 for x in STEPS for y in STEPS}
    rows_of = {(y, z): lax.rem(up[y], 2) * 4 + deep[z] for y in STEPS for z in STEPS}

    def peer(v):
        x, y, z = v
        prow, pcol = rows_of[y, z], cols[x, y]
        return prow * COLC + pcol, (prow, pcol * 2 + core)

    load_pair = pltpu.make_async_copy(pair_hbm, raw, io_sem.at[0])
    load_pair.start()
    load_cot = pltpu.make_async_copy(cot_hbm, cot, io_sem.at[1])
    load_cot.start()

    barrier = pltpu.get_barrier_semaphore()
    for v in NEAR:
        pl.semaphore_signal(barrier, inc=1, device_id=peer(v)[1], device_id_type=MESH)
    pl.semaphore_signal(barrier, inc=1, device_id=sibling, device_id_type=MESH)

    def keep(src_of, dst, recv):
        pltpu.make_async_copy(src_of(me), dst, recv).start()

    def exchange(src_of, dst, send, recv, others=OTHERS):
        for v in others:
            q, device = peer(v)
            pltpu.make_async_remote_copy(
                src_ref=src_of(q),
                dst_ref=dst,
                send_sem=send,
                recv_sem=recv,
                device_id=device,
                device_id_type=MESH,
            ).start()

    def arrived(buf, sem):
        pltpu.make_async_copy(buf, buf, sem).wait()

    def sent(buf, sem):
        part = buf.at[pl.ds(0, PEERS - 1)]
        pltpu.make_async_copy(part, part, sem).wait()

    wcat[:HID] = wl_ref[...]
    wcat[HID:] = wlg_ref[...]
    eye = lax.broadcasted_iota(jnp.int32, (HID, HID), 0) == lax.broadcasted_iota(jnp.int32, (HID, HID), 1)
    column = jnp.sum(jnp.where(eye, gain_ref[...], 0.0), axis=1, keepdims=True)
    gcol[...] = jnp.broadcast_to(column, (HID, LANES))

    load_pair.wait()

    def stage_rows(t, n):
        return pl.ds(t * (HID * SB) + n, HID, stride=SB)

    def steps(step, t):
        lax.fori_loop(0, SB, lambda n, _: (step(t, n), 0)[1], 0, unroll=UNROLL)

    def left_step(t, n):
        s = t * SB + n
        x = jnp.concatenate([raw[s], raw[s + HALF]], axis=0)
        centred = x - jnp.mean(x, -1, keepdims=True)
        inv_std = lax.rsqrt(jnp.mean(centred * centred, -1, keepdims=True) + EPS)
        normed = centred * inv_std
        xn[s] = normed[:SIDE]
        xn[s + HALF] = normed[SIDE:]
        inv[s] = jnp.broadcast_to(inv_std, (LANES, CH))
        both = dot(wcat[...], normed.astype(BF16), 1, 1)
        value = both[:HID]
        left_sig = jax.nn.sigmoid(both[HID:])
        val[s] = value
        sig[s] = left_sig
        stage[stage_rows(t, n), :] = left_sig * value

    def stage_block(t, h):
        return pl.ds(pl.multiple_of((t * HID + h) * SB, SB), SB)

    def project_left(t):
        steps(left_step, t)

        def pack_left(h, _):
            send_l[t, h] = stage[stage_block(t, h), :].astype(BF16)
            return 0

        lax.fori_loop(0, HID, pack_left, 0, unroll=8)

    def send_left(t):
        keep(lambda q: send_l.at[t, q], lb.at[t, core, me], tri_sem.at[9, t])
        exchange(lambda q: send_l.at[t, q], lb.at[t, core, me], tri_sem.at[8, t], tri_sem.at[9, t])

    project_left(0)
    pl.semaphore_wait(barrier, len(NEAR) + 1)
    exchange(lambda q: right_hbm.at[q], rt.at[me], send_sem.at[0], line_sem, LINE)
    keep(lambda q: right_hbm.at[q], rt.at[me], recv_sem.at[0])
    project_left(1)
    arrived(rt.at[pl.ds(0, len(LINE))], line_sem)
    send_left(0)
    exchange(lambda q: right_hbm.at[q], rt.at[me], send_sem.at[0], recv_sem.at[0], REST)

    def gate_step(s, _):
        low = jnp.concatenate([xn[s], xn[s + HALF]], axis=0).astype(BF16)
        gate[s] = jax.nn.sigmoid(dot(low, wg_ref[...], 1, 0))
        return 0

    lax.fori_loop(0, HALF, gate_step, 0, unroll=UNROLL)

    def swap_left(t):
        return pltpu.make_async_remote_copy(
            src_ref=lb.at[t, core],
            dst_ref=lb.at[t, core],
            send_sem=tri_sem.at[10, t],
            recv_sem=tri_sem.at[11, t],
            device_id=sibling,
            device_id_type=MESH,
        )

    def take_left(t):
        arrived(lb.at[t, core], tri_sem.at[9, t])
        swap_left(t).start()
        arrived(lb.at[t, 1 - core], tri_sem.at[11, t])

        def unpack_left(q, _):
            r, c = q // COLC, lax.rem(q, COLC)
            top, bottom = swap(lb[t, 0, q].astype(F32), lb[t, 1, q].astype(F32))
            block = jnp.concatenate([top, bottom], axis=0).astype(BF16)
            lfull[c, pl.ds(pl.multiple_of(t * TR + r * 2 * SB, 2 * SB), 2 * SB), :] = block
            return 0

        lax.fori_loop(0, PEERS, unpack_left, 0, unroll=8)

    def k_left(lo, rows=slice(None)):
        return jnp.concatenate([lfull[lo, rows], lfull[lo + 1, rows]], axis=1)

    def k_right(lo):
        a = jnp.concatenate([rt[lo * COLC + c] for c in range(COLC)], axis=0)
        b = jnp.concatenate([rt[(lo + 1) * COLC + c] for c in range(COLC)], axis=0)
        return jnp.concatenate([a, b], axis=1)

    send_left(1)
    take_left(0)
    sent(right_hbm, send_sem.at[0])
    arrived(rt.at[pl.ds(0, PEERS - len(LINE))], recv_sem.at[0])

    for t in range(NCH):
        if t:
            take_left(t)
        rows = slice(t * TR, (t + 1) * TR)
        total = dot(k_left(0, rows), k_right(0), 1, 1)
        for lo in range(2, ROW, 2):
            total += dot(k_left(lo, rows), k_right(lo), 1, 1)
        for r in range(ROW):
            for p in range(COLC // 2):
                lanes = slice(p * LANES, (p + 1) * LANES)
                a, b = swap(
                    total[r * 2 * SB : r * 2 * SB + SB, lanes],
                    total[r * 2 * SB + SB : (r + 1) * 2 * SB, lanes],
                )
                tm[t, r * COLC + 2 * p] = a.astype(BF16)
                tm[t, r * COLC + 2 * p + 1] = b.astype(BF16)
        keep(lambda q: tm.at[t, q], tr.at[t, me], tri_sem.at[1, t])
        exchange(lambda q: tm.at[t, q], tr.at[t, me], tri_sem.at[0, t], tri_sem.at[1, t])

    def widen(buf, t):
        def one(h, _):
            stage[stage_block(t, h), :] = buf[t, h].astype(F32)
            return 0

        lax.fori_loop(0, HID, one, 0, unroll=8)

    def middle_step(t, n):
        s = t * SB + n
        tri = stage[stage_rows(t, n), :]
        centred = tri - jnp.mean(tri, 0, keepdims=True)
        inv_out = lax.rsqrt(jnp.mean(centred * centred, 0, keepdims=True) + EPS)
        hat = centred * inv_out
        gain = gcol[...]
        linear = dot((hat * gain).astype(BF16), wo_ref[...], 0, 0)
        g = gate[s]
        update = g * linear
        upd[s] = update[:SIDE]
        upd[s + HALF] = update[SIDE:]
        ct = jnp.concatenate([cot[s], cot[s + HALF]], axis=0)
        d_linear = ct * g
        dgate[s] = (ct * linear * g * (1.0 - g)).astype(BF16)
        d_scaled = dot(wo_ref[...], d_linear.astype(BF16), 1, 1) * gain
        d_tri = inv_out * (
            d_scaled
            - jnp.mean(d_scaled, 0, keepdims=True)
            - hat * jnp.mean(d_scaled * hat, 0, keepdims=True)
        )
        stage_d[stage_rows(t, n), :] = d_tri

    load_cot.wait()
    for t in range(NCH):
        arrived(tr.at[t], tri_sem.at[1, t])
        widen(tr, t)
        steps(middle_step, t)

        def pack_tri(h, _):
            dts[t, h] = stage_d[stage_block(t, h), :].astype(BF16)
            return 0

        lax.fori_loop(0, HID, pack_tri, 0, unroll=8)
        keep(lambda q: dts.at[t, q], dtr.at[t, me], tri_sem.at[3, t])
        exchange(lambda q: dts.at[t, q], dtr.at[t, me], tri_sem.at[2, t], tri_sem.at[3, t])

    def swap_grad(t):
        return pltpu.make_async_remote_copy(
            src_ref=dlx.at[t],
            dst_ref=dly.at[t],
            send_sem=tri_sem.at[4, t],
            recv_sem=tri_sem.at[5, t],
            device_id=sibling,
            device_id_type=MESH,
        )

    def tri_grad(t):
        arrived(dtr.at[t], tri_sem.at[3, t])

        def unpack_tri(n, _):
            r, p = n // (COLC // 2), lax.rem(n, COLC // 2)
            at = r * COLC + 2 * p
            top, bottom = swap(dtr[t, at].astype(F32), dtr[t, at + 1].astype(F32))
            block = jnp.concatenate([top, bottom], axis=0).astype(BF16)
            dtfull[p, pl.ds(pl.multiple_of(t * TR + r * 2 * SB, 2 * SB), 2 * SB), :] = block
            return 0

        lax.fori_loop(0, PEERS // 2, unpack_tri, 0, unroll=8)

    def left_grad(t):
        d_tri = jnp.concatenate([dtfull[p, t * TR : (t + 1) * TR] for p in range(COLC // 2)], axis=1)
        for lo in range(0, ROW, 2):
            part = dot(d_tri, k_right(lo), 1, 0)
            for c in range(2):
                for r in range(ROW):
                    lanes = slice(c * LANES, (c + 1) * LANES)
                    for_0, for_1 = swap(
                        part[r * 2 * SB : r * 2 * SB + SB, lanes],
                        part[r * 2 * SB + SB : (r + 1) * 2 * SB, lanes],
                    )
                    at = r * COLC + lo + c
                    first = core == 0
                    dlk[t, at] = jnp.where(first, for_0, for_1)
                    dlx[t, at] = jnp.where(first, for_1, for_0).astype(BF16)
        swap_grad(t).start()

    def send_left_grad(t):
        swap_grad(t).wait_recv()

        def add_halves(q, _):
            dls[t, q] = (dlk[t, q] + dly[t, q].astype(F32)).astype(BF16)
            return 0

        lax.fori_loop(0, PEERS, add_halves, 0, unroll=8)
        keep(lambda q: dls.at[t, q], dlr.at[t, me], tri_sem.at[7, t])
        exchange(lambda q: dls.at[t, q], dlr.at[t, me], tri_sem.at[6, t], tri_sem.at[7, t])

    def right_grad(t):
        rows = slice(t * TR, (t + 1) * TR)
        d_tri = jnp.concatenate([dtfull[p, rows] for p in range(COLC // 2)], axis=1)
        for lo in range(0, COLC, 2):
            part = dot(d_tri, k_left(lo, rows), 0, 0)
            if t:
                part += grsum[lo // 2]
            if t < NCH - 1:
                grsum[lo // 2] = part
                continue
            part = part.astype(BF16)
            for c in range(2):
                for cc in range(COLC):
                    grs[(lo + c) * COLC + cc] = part[cc * SIDE : (cc + 1) * SIDE, c * LANES : (c + 1) * LANES]

    for t in range(NCH - 1):
        tri_grad(t)
        left_grad(t)
        right_grad(t)
        send_left_grad(t)
    tri_grad(NCH - 1)

    right_grad(NCH - 1)

    def send_right_grad(others):
        exchange(lambda q: grs.at[q], gr.at[me], send_sem.at[3], recv_sem.at[3], others)

    keep(lambda q: grs.at[q], gr.at[me], recv_sem.at[3])
    send_right_grad(OTHERS[0::4])
    left_grad(NCH - 1)
    send_left_grad(NCH - 1)
    send_right_grad([v for n, v in enumerate(OTHERS) if n % 4])

    def final_step(t, n):
        s = t * SB + n
        d_left = stage[stage_rows(t, n), :]
        left_sig, value = sig[s], val[s]
        d_value = d_left * left_sig
        d_logit = d_left * value * left_sig * (1.0 - left_sig)
        stacked = jnp.concatenate([d_value, d_logit], axis=0).astype(BF16)
        grad = dot(stacked, wcat[...], 0, 0) + dot(dgate[s], wg_ref[...], 1, 1)
        normed = jnp.concatenate([xn[s], xn[s + HALF]], axis=0)
        out = inv[s] * (
            grad
            - jnp.mean(grad, -1, keepdims=True)
            - normed * jnp.mean(grad * normed, -1, keepdims=True)
        )
        gp[s] = out[:SIDE]
        gp[s + HALF] = out[SIDE:]

    for t in range(NCH):
        arrived(dlr.at[t], tri_sem.at[7, t])
        widen(dlr, t)
        steps(final_step, t)

    for t in range(NCH):
        sent(dts.at[t], tri_sem.at[2, t])
        swap_grad(t).wait_send()
        sent(send_l.at[t], tri_sem.at[8, t])
        swap_left(t).wait_send()
    for t in range(NCH):
        sent(tm.at[t], tri_sem.at[0, t])
    for t in range(NCH):
        sent(dls.at[t], tri_sem.at[6, t])
    sent(grs, send_sem.at[3])
    arrived(gr, recv_sem.at[3])


def store(upd, gp, gr, upd_out, gp_out, gr_out, sem):
    copies = [
        pltpu.make_async_copy(src, dst, sem.at[n])
        for n, (src, dst) in enumerate(((upd, upd_out), (gp, gp_out), (gr, gr_out)))
    ]
    for copy in copies:
        copy.start()
    for copy in copies:
        copy.wait()


def shards(pair, right_proj, w_left_gate, w_left, w_gate, out_gain, w_out, cotangent):
    any_spec = pl.BlockSpec(memory_space=pl.ANY)
    vmem = pl.BlockSpec(memory_space=pltpu.VMEM)
    cells = (SIDE, SIDE, CH)
    chunks = (NCH, PEERS, SB, LANES)
    block16 = (PEERS, SIDE, KB)
    per_step = (HALF, LANES, CH)
    heads = (HALF, HID, LANES)
    scratch = [
        (cells, F32), (cells, F32), (cells, F32), (per_step, F32), (per_step, F32), (heads, F32), (heads, F32),
        (per_step, BF16),
        ((HID * HALF, LANES), F32), ((HID * HALF, LANES), F32),
        (chunks, BF16),
        ((NCH, 2, PEERS, SB, LANES), BF16),
        ((COLC, ROW * SIDE, LANES), BF16),
        (block16, BF16),
        (chunks, BF16), (chunks, BF16), (chunks, BF16), (chunks, BF16),
        ((COLC // 2, ROW * SIDE, LANES), BF16),
        ((COLC // 2, COLC * SIDE, 2 * LANES), F32),
        (block16, BF16),
        (chunks, F32),
        (chunks, BF16), (chunks, BF16), (chunks, BF16), (chunks, BF16),
        ((2 * HID, CH), BF16),
        ((HID, LANES), F32),
    ]
    update, grad_pair, grad_right = pl.pallas_call(
        kernel,
        out_shape=(pltpu.VMEM(cells, F32), pltpu.VMEM(cells, F32), pltpu.VMEM((HID, SIDE, KB), BF16)),
        in_specs=[any_spec, any_spec, vmem, vmem, vmem, vmem, vmem, any_spec],
        out_specs=(vmem, vmem, vmem),
        scratch_shapes=[pltpu.VMEM(shape, dtype) for shape, dtype in scratch]
        + [
            pltpu.SemaphoreType.DMA((2,)),
            pltpu.SemaphoreType.DMA((4,)),
            pltpu.SemaphoreType.DMA((4,)),
            pltpu.SemaphoreType.DMA((12, NCH)),
            pltpu.SemaphoreType.DMA,
        ],
        compiler_params=pltpu.CompilerParams(
            collective_id=0, has_side_effects=True, vmem_limit_bytes=58 * 1024 * 1024
        ),
    )(
        pair,
        jnp.transpose(right_proj, (0, 2, 1)),
        w_left_gate.T,
        w_left.T,
        w_gate,
        out_gain.reshape(1, HID),
        w_out,
        cotangent,
    )
    update, grad_pair, grad_right = pl.pallas_call(
        store,
        out_shape=(
            jax.ShapeDtypeStruct(cells, F32),
            jax.ShapeDtypeStruct(cells, F32),
            jax.ShapeDtypeStruct((HID, SIDE, KB), BF16),
        ),
        in_specs=[vmem, vmem, vmem],
        out_specs=(any_spec, any_spec, any_spec),
        scratch_shapes=[pltpu.SemaphoreType.DMA((3,))],
        compiler_params=pltpu.CompilerParams(vmem_limit_bytes=1024 * 1024),
    )(*(pltpu.with_memory_space_constraint(a, pltpu.VMEM) for a in (update, grad_pair, grad_right)))
    return update, grad_pair, jnp.transpose(grad_right, (0, 2, 1))


def solution(mesh):
    in_specs = (
        P("row", "col", None),
        P(None, "row", "col"),
        P(),
        P(),
        P(),
        P(),
        P(),
        P("row", "col", None),
    )
    out_specs = (P("row", "col", None), P("row", "col", None), P(None, "row", "col"))
    return jax.shard_map(shards, mesh=mesh, in_specs=in_specs, out_specs=out_specs, check_vma=False)
```

```python
import random

import jax
import jax.numpy as jnp
from jax import lax
from jax.experimental import pallas as pl
from jax.experimental.pallas import tpu as pltpu
from jax.sharding import PartitionSpec as P

EPS = 1e-05
F32 = jnp.float32
BF16 = jnp.bfloat16
MESH = pl.DeviceIdType.MESH

CH = 128
HID = 64
SIDE = 64
ROW = 8
COLC = 8
HALF = SIDE // 2
KB = 128
LANES = 128
PEERS = ROW * COLC
NCH = 2
SB = HALF // NCH
TR = ROW * 2 * SB
UNROLL = 16
STEPS = (0, 1, 2, -1)
OTHERS = [(x, y, z) for x in STEPS for y in STEPS for z in STEPS if (x, y, z) != (0, 0, 0)]
random.Random(1).shuffle(OTHERS)
OTHERS.sort(key=lambda v: -sum(map(abs, v)))
PLANE = [v for v in OTHERS if v[2] == 0]
LINE = [v for v in OTHERS if v[0] == 0 and v[1] == 0]
NEAR = [v for v in OTHERS if v in PLANE or v in LINE]
REST = [v for v in OTHERS if v not in LINE]


def dot(a, b, da, db):
    return lax.dot_general(a, b, (((da,), (db,)), ((), ())), preferred_element_type=F32)


def swap(a, b):
    left = lax.broadcasted_iota(jnp.int32, a.shape, a.ndim - 1) < LANES // 2
    ra = pltpu.roll(a, LANES // 2, a.ndim - 1)
    rb = pltpu.roll(b, LANES // 2, b.ndim - 1)
    return jnp.where(left, a, rb), jnp.where(left, ra, b)


def kernel(
    pair_hbm, right_hbm, wlg_ref, wl_ref, wg_ref, gain_ref, wo_ref, cot_hbm,
    upd, gp, gr,
    raw, xn, cot, inv, gate, sig, val, dgate,
    stage, stage_d, send_l, lb, lfull, rt, tm, tr, dts, dtr, dtfull, grsum, grs, dlk, dlx, dly, dls, dlr, wcat, gcol,
    io_sem, send_sem, recv_sem, tri_sem, line_sem,
):
    row, col = lax.axis_index("row"), lax.axis_index("col")
    core = lax.rem(col, 2)
    colc = col // 2
    me = row * COLC + colc
    sibling = (row, colc * 2 + (1 - core))

    across = {d: lax.rem(colc // 2 + d + 4, 4) for d in STEPS}
    up = {d: lax.rem(lax.rem(colc, 2) * 2 + row // 4 + d + 4, 4) for d in STEPS}
    deep = {d: lax.rem(lax.rem(row, 4) + d + 4, 4) for d in STEPS}
    cols = {(x, y): across[x] * 2 + up[y] // 2 for x in STEPS for y in STEPS}
    rows_of = {(y, z): lax.rem(up[y], 2) * 4 + deep[z] for y in STEPS for z in STEPS}

    def peer(v):
        x, y, z = v
        prow, pcol = rows_of[y, z], cols[x, y]
        return prow * COLC + pcol, (prow, pcol * 2 + core)

    load_pair = pltpu.make_async_copy(pair_hbm, raw, io_sem.at[0])
    load_pair.start()
    load_cot = pltpu.make_async_copy(cot_hbm, cot, io_sem.at[1])
    load_cot.start()

    barrier = pltpu.get_barrier_semaphore()
    for v in NEAR:
        pl.semaphore_signal(barrier, inc=1, device_id=peer(v)[1], device_id_type=MESH)
    pl.semaphore_signal(barrier, inc=1, device_id=sibling, device_id_type=MESH)

    def keep(src_of, dst, recv):
        pltpu.make_async_copy(src_of(me), dst, recv).start()

    def exchange(src_of, dst, send, recv, others=OTHERS):
        for v in others:
            q, device = peer(v)
            pltpu.make_async_remote_copy(
                src_ref=src_of(q),
                dst_ref=dst,
                send_sem=send,
                recv_sem=recv,
                device_id=device,
                device_id_type=MESH,
            ).start()

    def arrived(buf, sem):
        pltpu.make_async_copy(buf, buf, sem).wait()

    def sent(buf, sem):
        part = buf.at[pl.ds(0, PEERS - 1)]
        pltpu.make_async_copy(part, part, sem).wait()

    wcat[:HID] = wl_ref[...]
    wcat[HID:] = wlg_ref[...]
    eye = lax.broadcasted_iota(jnp.int32, (HID, HID), 0) == lax.broadcasted_iota(jnp.int32, (HID, HID), 1)
    column = jnp.sum(jnp.where(eye, gain_ref[...], 0.0), axis=1, keepdims=True)
    gcol[...] = jnp.broadcast_to(column, (HID, LANES))

    load_pair.wait()

    def stage_rows(t, n):
        return pl.ds(t * (HID * SB) + n, HID, stride=SB)

    def steps(step, t):
        lax.fori_loop(0, SB, lambda n, _: (step(t, n), 0)[1], 0, unroll=UNROLL)

    def left_step(t, n):
        s = t * SB + n
        x = jnp.concatenate([raw[s], raw[s + HALF]], axis=0)
        centred = x - jnp.mean(x, -1, keepdims=True)
        inv_std = lax.rsqrt(jnp.mean(centred * centred, -1, keepdims=True) + EPS)
        normed = centred * inv_std
        xn[s] = normed[:SIDE]
        xn[s + HALF] = normed[SIDE:]
        inv[s] = jnp.broadcast_to(inv_std, (LANES, CH))
        both = dot(wcat[...], normed.astype(BF16), 1, 1)
        value = both[:HID]
        left_sig = jax.nn.sigmoid(both[HID:])
        val[s] = value
        sig[s] = left_sig
        stage[stage_rows(t, n), :] = left_sig * value

    def stage_block(t, h):
        return pl.ds(pl.multiple_of((t * HID + h) * SB, SB), SB)

    def project_left(t):
        steps(left_step, t)

        def pack_left(h, _):
            send_l[t, h] = stage[stage_block(t, h), :].astype(BF16)
            return 0

        lax.fori_loop(0, HID, pack_left, 0, unroll=8)

    def send_left(t):
        keep(lambda q: send_l.at[t, q], lb.at[t, core, me], tri_sem.at[9, t])
        exchange(lambda q: send_l.at[t, q], lb.at[t, core, me], tri_sem.at[8, t], tri_sem.at[9, t])

    project_left(0)
    pl.semaphore_wait(barrier, len(NEAR) + 1)
    exchange(lambda q: right_hbm.at[q], rt.at[me], send_sem.at[0], line_sem, LINE)
    keep(lambda q: right_hbm.at[q], rt.at[me], recv_sem.at[0])
    project_left(1)
    arrived(rt.at[pl.ds(0, len(LINE))], line_sem)
    send_left(0)
    exchange(lambda q: right_hbm.at[q], rt.at[me], send_sem.at[0], recv_sem.at[0], REST)

    def gate_step(s, _):
        low = jnp.concatenate([xn[s], xn[s + HALF]], axis=0).astype(BF16)
        gate[s] = jax.nn.sigmoid(dot(low, wg_ref[...], 1, 0))
        return 0

    lax.fori_loop(0, HALF, gate_step, 0, unroll=UNROLL)

    def swap_left(t):
        return pltpu.make_async_remote_copy(
            src_ref=lb.at[t, core],
            dst_ref=lb.at[t, core],
            send_sem=tri_sem.at[10, t],
            recv_sem=tri_sem.at[11, t],
            device_id=sibling,
            device_id_type=MESH,
        )

    def take_left(t):
        arrived(lb.at[t, core], tri_sem.at[9, t])
        swap_left(t).start()
        arrived(lb.at[t, 1 - core], tri_sem.at[11, t])

        def unpack_left(q, _):
            r, c = q // COLC, lax.rem(q, COLC)
            top, bottom = swap(lb[t, 0, q].astype(F32), lb[t, 1, q].astype(F32))
            block = jnp.concatenate([top, bottom], axis=0).astype(BF16)
            lfull[c, pl.ds(pl.multiple_of(t * TR + r * 2 * SB, 2 * SB), 2 * SB), :] = block
            return 0

        lax.fori_loop(0, PEERS, unpack_left, 0, unroll=8)

    def k_left(lo, rows=slice(None)):
        return jnp.concatenate([lfull[lo, rows], lfull[lo + 1, rows]], axis=1)

    def k_right(lo):
        a = jnp.concatenate([rt[lo * COLC + c] for c in range(COLC)], axis=0)
        b = jnp.concatenate([rt[(lo + 1) * COLC + c] for c in range(COLC)], axis=0)
        return jnp.concatenate([a, b], axis=1)

    send_left(1)
    take_left(0)
    sent(right_hbm, send_sem.at[0])
    arrived(rt.at[pl.ds(0, PEERS - len(LINE))], recv_sem.at[0])

    for t in range(NCH):
        if t:
            take_left(t)
        rows = slice(t * TR, (t + 1) * TR)
        total = dot(k_left(0, rows), k_right(0), 1, 1)
        for lo in range(2, ROW, 2):
            total += dot(k_left(lo, rows), k_right(lo), 1, 1)
        for r in range(ROW):
            for p in range(COLC // 2):
                lanes = slice(p * LANES, (p + 1) * LANES)
                a, b = swap(
                    total[r * 2 * SB : r * 2 * SB + SB, lanes],
                    total[r * 2 * SB + SB : (r + 1) * 2 * SB, lanes],
                )
                tm[t, r * COLC + 2 * p] = a.astype(BF16)
                tm[t, r * COLC + 2 * p + 1] = b.astype(BF16)
        if t:
            sent(tm.at[t - 1], tri_sem.at[0, t - 1])
        keep(lambda q: tm.at[t, q], tr.at[t, me], tri_sem.at[1, t])
        exchange(lambda q: tm.at[t, q], tr.at[t, me], tri_sem.at[0, t], tri_sem.at[1, t])

    def widen(buf, t):
        def one(h, _):
            stage[stage_block(t, h), :] = buf[t, h].astype(F32)
            return 0

        lax.fori_loop(0, HID, one, 0, unroll=8)

    def middle_step(t, n):
        s = t * SB + n
        tri = stage[stage_rows(t, n), :]
        centred = tri - jnp.mean(tri, 0, keepdims=True)
        inv_out = lax.rsqrt(jnp.mean(centred * centred, 0, keepdims=True) + EPS)
        hat = centred * inv_out
        gain = gcol[...]
        linear = dot((hat * gain).astype(BF16), wo_ref[...], 0, 0)
        g = gate[s]
        update = g * linear
        upd[s] = update[:SIDE]
        upd[s + HALF] = update[SIDE:]
        ct = jnp.concatenate([cot[s], cot[s + HALF]], axis=0)
        d_linear = ct * g
        dgate[s] = (ct * linear * g * (1.0 - g)).astype(BF16)
        d_scaled = dot(wo_ref[...], d_linear.astype(BF16), 1, 1) * gain
        d_tri = inv_out * (
            d_scaled
            - jnp.mean(d_scaled, 0, keepdims=True)
            - hat * jnp.mean(d_scaled * hat, 0, keepdims=True)
        )
        stage_d[stage_rows(t, n), :] = d_tri

    load_cot.wait()
    for t in range(NCH):
        arrived(tr.at[t], tri_sem.at[1, t])
        widen(tr, t)
        steps(middle_step, t)

        def pack_tri(h, _):
            dts[t, h] = stage_d[stage_block(t, h), :].astype(BF16)
            return 0

        lax.fori_loop(0, HID, pack_tri, 0, unroll=8)
        keep(lambda q: dts.at[t, q], dtr.at[t, me], tri_sem.at[3, t])
        exchange(lambda q: dts.at[t, q], dtr.at[t, me], tri_sem.at[2, t], tri_sem.at[3, t])

    def swap_grad(t):
        return pltpu.make_async_remote_copy(
            src_ref=dlx.at[t],
            dst_ref=dly.at[t],
            send_sem=tri_sem.at[4, t],
            recv_sem=tri_sem.at[5, t],
            device_id=sibling,
            device_id_type=MESH,
        )

    def tri_grad(t):
        arrived(dtr.at[t], tri_sem.at[3, t])

        def unpack_tri(n, _):
            r, p = n // (COLC // 2), lax.rem(n, COLC // 2)
            at = r * COLC + 2 * p
            top, bottom = swap(dtr[t, at].astype(F32), dtr[t, at + 1].astype(F32))
            block = jnp.concatenate([top, bottom], axis=0).astype(BF16)
            dtfull[p, pl.ds(pl.multiple_of(t * TR + r * 2 * SB, 2 * SB), 2 * SB), :] = block
            return 0

        lax.fori_loop(0, PEERS // 2, unpack_tri, 0, unroll=8)

    def left_grad(t):
        d_tri = jnp.concatenate([dtfull[p, t * TR : (t + 1) * TR] for p in range(COLC // 2)], axis=1)
        for lo in range(0, ROW, 2):
            part = dot(d_tri, k_right(lo), 1, 0)
            for c in range(2):
                for r in range(ROW):
                    lanes = slice(c * LANES, (c + 1) * LANES)
                    for_0, for_1 = swap(
                        part[r * 2 * SB : r * 2 * SB + SB, lanes],
                        part[r * 2 * SB + SB : (r + 1) * 2 * SB, lanes],
                    )
                    at = r * COLC + lo + c
                    first = core == 0
                    dlk[t, at] = jnp.where(first, for_0, for_1)
                    dlx[t, at] = jnp.where(first, for_1, for_0).astype(BF16)
        swap_grad(t).start()

    def send_left_grad(t):
        swap_grad(t).wait_recv()

        def add_halves(q, _):
            dls[t, q] = (dlk[t, q] + dly[t, q].astype(F32)).astype(BF16)
            return 0

        lax.fori_loop(0, PEERS, add_halves, 0, unroll=8)
        keep(lambda q: dls.at[t, q], dlr.at[t, me], tri_sem.at[7, t])
        exchange(lambda q: dls.at[t, q], dlr.at[t, me], tri_sem.at[6, t], tri_sem.at[7, t])

    def right_grad(t):
        rows = slice(t * TR, (t + 1) * TR)
        d_tri = jnp.concatenate([dtfull[p, rows] for p in range(COLC // 2)], axis=1)
        for lo in range(0, COLC, 2):
            part = dot(d_tri, k_left(lo, rows), 0, 0)
            if t:
                part += grsum[lo // 2]
            if t < NCH - 1:
                grsum[lo // 2] = part
                continue
            part = part.astype(BF16)
            for c in range(2):
                for cc in range(COLC):
                    grs[(lo + c) * COLC + cc] = part[cc * SIDE : (cc + 1) * SIDE, c * LANES : (c + 1) * LANES]

    for t in range(NCH - 1):
        tri_grad(t)
        left_grad(t)
        right_grad(t)
        send_left_grad(t)
    tri_grad(NCH - 1)

    right_grad(NCH - 1)

    def send_right_grad(others):
        exchange(lambda q: grs.at[q], gr.at[me], send_sem.at[3], recv_sem.at[3], others)

    keep(lambda q: grs.at[q], gr.at[me], recv_sem.at[3])
    send_right_grad(OTHERS[0::8])
    left_grad(NCH - 1)
    send_left_grad(NCH - 1)
    send_right_grad([v for n, v in enumerate(OTHERS) if n % 8])

    def final_step(t, n):
        s = t * SB + n
        d_left = stage[stage_rows(t, n), :]
        left_sig, value = sig[s], val[s]
        d_value = d_left * left_sig
        d_logit = d_left * value * left_sig * (1.0 - left_sig)
        stacked = jnp.concatenate([d_value, d_logit], axis=0).astype(BF16)
        grad = dot(stacked, wcat[...], 0, 0) + dot(dgate[s], wg_ref[...], 1, 1)
        normed = jnp.concatenate([xn[s], xn[s + HALF]], axis=0)
        out = inv[s] * (
            grad
            - jnp.mean(grad, -1, keepdims=True)
            - normed * jnp.mean(grad * normed, -1, keepdims=True)
        )
        gp[s] = out[:SIDE]
        gp[s + HALF] = out[SIDE:]

    for t in range(NCH):
        arrived(dlr.at[t], tri_sem.at[7, t])
        widen(dlr, t)
        steps(final_step, t)

    for t in range(NCH):
        sent(dts.at[t], tri_sem.at[2, t])
        swap_grad(t).wait_send()
        sent(send_l.at[t], tri_sem.at[8, t])
        swap_left(t).wait_send()
    sent(tm.at[NCH - 1], tri_sem.at[0, NCH - 1])
    for t in range(NCH):
        sent(dls.at[t], tri_sem.at[6, t])
    sent(grs, send_sem.at[3])
    arrived(gr, recv_sem.at[3])


def store(upd, gp, gr, upd_out, gp_out, gr_out, sem):
    copies = [
        pltpu.make_async_copy(src, dst, sem.at[n])
        for n, (src, dst) in enumerate(((upd, upd_out), (gp, gp_out), (gr, gr_out)))
    ]
    for copy in copies:
        copy.start()
    for copy in copies:
        copy.wait()


def shards(pair, right_proj, w_left_gate, w_left, w_gate, out_gain, w_out, cotangent):
    any_spec = pl.BlockSpec(memory_space=pl.ANY)
    vmem = pl.BlockSpec(memory_space=pltpu.VMEM)
    cells = (SIDE, SIDE, CH)
    chunks = (NCH, PEERS, SB, LANES)
    block16 = (PEERS, SIDE, KB)
    per_step = (HALF, LANES, CH)
    heads = (HALF, HID, LANES)
    scratch = [
        (cells, F32), (cells, F32), (cells, F32), (per_step, F32), (per_step, F32), (heads, F32), (heads, F32),
        (per_step, BF16),
        ((HID * HALF, LANES), F32), ((HID * HALF, LANES), F32),
        (chunks, BF16),
        ((NCH, 2, PEERS, SB, LANES), BF16),
        ((COLC, ROW * SIDE, LANES), BF16),
        (block16, BF16),
        (chunks, BF16), (chunks, BF16), (chunks, BF16), (chunks, BF16),
        ((COLC // 2, ROW * SIDE, LANES), BF16),
        ((COLC // 2, COLC * SIDE, 2 * LANES), F32),
        (block16, BF16),
        (chunks, F32),
        (chunks, BF16), (chunks, BF16), (chunks, BF16), (chunks, BF16),
        ((2 * HID, CH), BF16),
        ((HID, LANES), F32),
    ]
    update, grad_pair, grad_right = pl.pallas_call(
        kernel,
        out_shape=(pltpu.VMEM(cells, F32), pltpu.VMEM(cells, F32), pltpu.VMEM((HID, SIDE, KB), BF16)),
        in_specs=[any_spec, any_spec, vmem, vmem, vmem, vmem, vmem, any_spec],
        out_specs=(vmem, vmem, vmem),
        scratch_shapes=[pltpu.VMEM(shape, dtype) for shape, dtype in scratch]
        + [
            pltpu.SemaphoreType.DMA((2,)),
            pltpu.SemaphoreType.DMA((4,)),
            pltpu.SemaphoreType.DMA((4,)),
            pltpu.SemaphoreType.DMA((12, NCH)),
            pltpu.SemaphoreType.DMA,
        ],
        compiler_params=pltpu.CompilerParams(
            collective_id=0, has_side_effects=True, vmem_limit_bytes=58 * 1024 * 1024
        ),
    )(
        pair,
        jnp.transpose(right_proj, (0, 2, 1)),
        w_left_gate.T,
        w_left.T,
        w_gate,
        out_gain.reshape(1, HID),
        w_out,
        cotangent,
    )
    update, grad_pair, grad_right = pl.pallas_call(
        store,
        out_shape=(
            jax.ShapeDtypeStruct(cells, F32),
            jax.ShapeDtypeStruct(cells, F32),
            jax.ShapeDtypeStruct((HID, SIDE, KB), BF16),
        ),
        in_specs=[vmem, vmem, vmem],
        out_specs=(any_spec, any_spec, any_spec),
        scratch_shapes=[pltpu.SemaphoreType.DMA((3,))],
        compiler_params=pltpu.CompilerParams(vmem_limit_bytes=1024 * 1024),
    )(*(pltpu.with_memory_space_constraint(a, pltpu.VMEM) for a in (update, grad_pair, grad_right)))
    return update, grad_pair, jnp.transpose(grad_right, (0, 2, 1))


def solution(mesh):
    in_specs = (
        P("row", "col", None),
        P(None, "row", "col"),
        P(),
        P(),
        P(),
        P(),
        P(),
        P("row", "col", None),
    )
    out_specs = (P("row", "col", None), P("row", "col", None), P(None, "row", "col"))
    return jax.shard_map(shards, mesh=mesh, in_specs=in_specs, out_specs=out_specs, check_vma=False)
```
